32 devices in a mesh: ctx: 8 (over z, y), fsdp: 4 (over x, core).
Axes of the slice: x: 2, y: 2, z: 4, core: 2. Of those that a mesh axis runs over, the one named last changes fastest.
Arguments:
- inputs: bfloat16 [16, 8, 2, 64, 960], P('fsdp', 'ctx'), may hold values from -6 to 6
- attn_gain: bfloat16 [960], P('fsdp'), may hold values from 0.099609375 to 1.8984375
- query_weight: bfloat16 [960, 960], P('fsdp'), may hold values from -0.1875 to 0.1875
- key_projection_weight: bfloat16 [960, 320], P('fsdp'), may hold values from -0.1875 to 0.1875
- value_projection_weight: bfloat16 [960, 320], P('fsdp'), may hold values from -0.1875 to 0.1875
- out_weight: bfloat16 [960, 960], P('fsdp'), may hold values from -1.5 to 1.5
- ffn_gain: bfloat16 [960], P('fsdp'), may hold values from 0.099609375 to 1.8984375
- gate_weight: bfloat16 [960, 2560], P('fsdp'), may hold values from -0.1875 to 0.1875
- up_weight: bfloat16 [960, 2560], P('fsdp'), may hold values from -0.1875 to 0.1875
- down_weight: bfloat16 [2560, 960], P('fsdp'), may hold values from -0.125 to 0.125
- positions: int32 [16, 8, 2, 64], P('fsdp', 'ctx'), may hold values from 0 to 2046, as said below
- cotangent: bfloat16 [16, 8, 2, 64, 960], P('fsdp', 'ctx'), may hold values from -6 to 6
Outputs:
- outputs: bfloat16 [16, 8, 2, 64, 960], P('fsdp', 'ctx')
- input_grad: float32 [16, 8, 2, 64, 960], P('fsdp', 'ctx')
- attn_gain_grad: float32 [960], P('fsdp')
- query_grad: float32 [960, 960], P('fsdp', 'ctx')
- key_grad: float32 [960, 320], P('fsdp', 'ctx')
- value_grad: float32 [960, 320], P('fsdp', 'ctx')
- out_grad: float32 [960, 960], P('fsdp', 'ctx')
- ffn_gain_grad: float32 [960], P('fsdp')
- gate_grad: float32 [960, 2560], P('fsdp', 'ctx')
- up_grad: float32 [960, 2560], P('fsdp', 'ctx')
- down_grad: float32 [2560, 960], P('fsdp', 'ctx')
The draws below stay inside these ranges and needn't reach their ends.
Inputs may be any that keep to these rules, and one draw needn't show every extreme that they name: `positions`: within each sequence, in token order, the first position is 0 and each next one is larger by 1 or 2.
All inputs are finite; a program needn't handle non-finite values.
Results may differ from the reference program's by a relative error of at most 0.019.
Values may be sent and summed in bfloat16 or wider, within the bound.
No kernel may reach another device: no remote copies, remote signals or barrier semaphores. Data moves between devices by JAX's collectives and lax.ppermute only.
A program may use at most 256 MiB of HBM per device.

```python
import jax
import jax.numpy as jnp
from jax import lax

MODEL_WIDTH = 960
FF = 2560
QUERY_HEADS = 15
KEY_VALUE_HEADS = 5
HEAD_SIZE = 64
BLK = 64
PAIRS = 8
SEQUENCE_LENGTH = 1024
SEQUENCE_COUNT = 16


def draw_positions(key, part):
    key = jax.random.fold_in(key, 7)
    steps = jax.random.randint(key, (SEQUENCE_COUNT, SEQUENCE_LENGTH), 1, 3)
    chosen = jax.random.randint(jax.random.fold_in(key, 11), (), 0, SEQUENCE_COUNT)
    widest = jnp.arange(SEQUENCE_COUNT)[:, None] == chosen
    steps = jnp.where(widest, 2, steps)
    first_column = jnp.arange(SEQUENCE_LENGTH)[None, :] == 0
    steps = jnp.where(first_column, 0, steps)
    natural = jnp.cumsum(steps, axis=1).reshape(SEQUENCE_COUNT, 2 * PAIRS, BLK)
    first = natural[:, :PAIRS]
    second = jnp.flip(natural[:, PAIRS:], axis=1)
    return jnp.stack([first, second], axis=2).astype(jnp.int32)


def strengthened(entries, own_key, source, target, parts, factor):
    owner, partner = [(jnp.arange(entries.shape[position]) // (entries.shape[position] // parts)).reshape([-1 if axis == position else 1 for axis in range(entries.ndim)]) for position in (source, target)]
    chosen = jax.random.permutation(own_key, parts)[partner]
    strong = (owner == chosen) | (owner == (partner + parts // 2) % parts)
    return jnp.where(strong, factor * entries, entries)


def levels(key, extent, split, smallest, high):
    level, own = 1.0, jax.random.fold_in(key, 6)
    for axis_at, blocks in split:
        steps = jnp.exp(jax.random.uniform(jax.random.fold_in(own, axis_at), (blocks,), jnp.float32, smallest / len(split), high / len(split)))
        level = level * jnp.repeat(steps, extent[axis_at] // blocks).reshape([-1 if axis == axis_at else 1 for axis in range(len(extent))])
    return level


def normal_values(key, dims, spread, bound, split=(), kind=jnp.bfloat16):
    loudness = levels(key, dims, split, -0.22, 0.18) if split else 1.0
    values = jax.random.normal(key, dims, jnp.float32) * spread * loudness
    return jnp.minimum(jnp.maximum(values, -bound), bound).astype(kind)


def noise_with(stream_key, dims, scale, bound, split, heavy, kind=jnp.bfloat16):
    values = scale * jax.random.normal(stream_key, dims, jnp.float32)
    if split:
        values = values * levels(stream_key, dims, split, -0.22, 0.18)
    return jnp.clip(strengthened(values, jax.random.fold_in(stream_key, 3), *heavy), -bound, bound).astype(kind)


def setup_inputs(seed: int = 0) -> dict:
    keys = jax.random.split(jax.random.key(seed), 13)
    inputs = normal_values(keys[0], (SEQUENCE_COUNT, PAIRS, 2, BLK, MODEL_WIDTH), 1.0, 6.0, ((0, 4), (1, 8)))
    attn_gain = jnp.clip(1.0 + 0.18 * jax.random.normal(keys[1], (MODEL_WIDTH,), jnp.float32), 0.099609375, 1.8984375).astype(jnp.bfloat16)
    query_weight = normal_values(keys[2], (MODEL_WIDTH, QUERY_HEADS * HEAD_SIZE), MODEL_WIDTH ** -0.5, 0.1875, ((0, 4),))
    key_projection_weight = normal_values(keys[3], (MODEL_WIDTH, KEY_VALUE_HEADS * HEAD_SIZE), MODEL_WIDTH ** -0.5, 0.1875, ((0, 4),))
    value_projection_weight = normal_values(keys[4], (MODEL_WIDTH, KEY_VALUE_HEADS * HEAD_SIZE), MODEL_WIDTH ** -0.5, 0.1875, ((0, 4),))
    out_weight = normal_values(keys[5], (QUERY_HEADS * HEAD_SIZE, MODEL_WIDTH), (QUERY_HEADS * HEAD_SIZE // 64) ** -0.5, 1.5, ((0, 4),))
    ffn_gain = jnp.clip(1.0 + 0.18 * jax.random.normal(keys[6], (MODEL_WIDTH,), jnp.float32), 0.099609375, 1.8984375).astype(jnp.bfloat16)
    gate_weight = normal_values(keys[7], (MODEL_WIDTH, FF), MODEL_WIDTH ** -0.5, 0.1875, ((0, 4),))
    up_weight = normal_values(keys[8], (MODEL_WIDTH, FF), MODEL_WIDTH ** -0.5, 0.1875, ((0, 4),))
    down_weight = normal_values(keys[9], (FF, MODEL_WIDTH), FF ** -0.5, 0.125, ((0, 4),))
    positions = draw_positions(jax.random.fold_in(keys[12], 71), 0)
    cotangent = noise_with(keys[11], (SEQUENCE_COUNT, PAIRS, 2, BLK, MODEL_WIDTH), 1.0, 6.0, ((0, 4), (1, 8)), (1, 4, 8, 2.0))
    return {"inputs": inputs, "attn_gain": attn_gain, "query_weight": query_weight, "key_projection_weight": key_projection_weight, "value_projection_weight": value_projection_weight, "out_weight": out_weight, "ffn_gain": ffn_gain, "gate_weight": gate_weight, "up_weight": up_weight, "down_weight": down_weight, "positions": positions, "cotangent": cotangent}


@jax.custom_vjp
def reduced_precision(v):
    return lax.optimization_barrier(v.astype(jnp.bfloat16)).astype(jnp.float32)

@jax.custom_vjp
def reduced_precision_back(v):
    return v

def low_keep(v):
    return (reduced_precision(v), None)

def low_pass(kept, grad):
    return (grad,)

def back_keep(v):
    return (v, None)

def back_low(kept, grad):
    return (reduced_precision(grad),)
reduced_precision.defvjp(low_keep, low_pass)
reduced_precision_back.defvjp(back_keep, back_low)
eps = 1e-05
theta_base = 100000.0

def to_natural(array):
    first = array[:, :, 0]
    second = jnp.flip(array[:, :, 1], axis=1)
    whole = jnp.concatenate([first, second], axis=1)
    return whole.reshape((array.shape[0], SEQUENCE_LENGTH) + array.shape[4:])

def to_pairs(array):
    blocks = array.reshape((array.shape[0], 2 * PAIRS, BLK) + array.shape[2:])
    first = blocks[:, :PAIRS]
    second = jnp.flip(blocks[:, PAIRS:], axis=1)
    return jnp.stack([first, second], axis=2)

def rope_tables(positions):
    half = HEAD_SIZE // 2
    freqs = theta_base ** (-jnp.arange(half, dtype=jnp.float32) * 2.0 / HEAD_SIZE)
    freqs = jnp.concatenate([freqs, freqs])
    angles = positions.astype(jnp.float32)[..., None, None] * freqs
    return (jnp.cos(angles), jnp.sin(angles))

def rotate(value_rows):
    half = value_rows.shape[-1] // 2
    return jnp.concatenate([-value_rows[..., half:], value_rows[..., :half]], axis=-1)

def rotate_pairs(value_rows, cosine_table, sine_table):
    return value_rows * cosine_table + rotate(value_rows) * sine_table

def rms_norm(value_rows, gain):
    return value_rows * lax.rsqrt(lax.optimization_barrier(jnp.mean(value_rows * value_rows, axis=-1, keepdims=True)) + eps) * gain

def project_rows(left_block, right_block):
    return jnp.einsum('bti,in->btn', left_block, right_block, precision=lax.Precision.HIGHEST)

def attend_whole(item):
    query_matrix, key_rows, value_rows = item
    grouped_heads = query_matrix.reshape(SEQUENCE_LENGTH, KEY_VALUE_HEADS, QUERY_HEADS // KEY_VALUE_HEADS, HEAD_SIZE)
    scores = jnp.einsum('qhgd,khd->hgqk', grouped_heads, key_rows, precision=lax.Precision.HIGHEST) * HEAD_SIZE ** (-0.5)
    scores = reduced_precision_back(scores)
    order = jnp.arange(SEQUENCE_LENGTH)
    allowed = order[None, :] <= order[:, None]
    scores = jnp.where(allowed, scores, -1e+30)
    probs = reduced_precision(jax.nn.softmax(scores, axis=-1))
    mixed = jnp.einsum('hgqk,khd->qhgd', probs, value_rows, precision=lax.Precision.HIGHEST)
    return mixed.reshape(SEQUENCE_LENGTH, QUERY_HEADS * HEAD_SIZE)

def reference(inputs, attn_gain, query_weight, key_projection_weight, value_projection_weight, out_weight, ffn_gain, gate_weight, up_weight, down_weight, positions, cotangent):
    cosine_table, sine_table = rope_tables(to_natural(positions))

    def forward(tokens, first_gain, query_w, key_matrix, value_matrix, out_w, second_gain, gate_w, up_w, down_w):
        normalized_input = reduced_precision(rms_norm(tokens, first_gain))
        query_matrix = reduced_precision_back(project_rows(normalized_input, query_w)).reshape(SEQUENCE_COUNT, SEQUENCE_LENGTH, QUERY_HEADS, HEAD_SIZE)
        query_matrix = reduced_precision(rotate_pairs(query_matrix, cosine_table, sine_table))
        key_rows = reduced_precision_back(project_rows(normalized_input, key_matrix)).reshape(SEQUENCE_COUNT, SEQUENCE_LENGTH, KEY_VALUE_HEADS, HEAD_SIZE)
        key_rows = reduced_precision(rotate_pairs(key_rows, cosine_table, sine_table))
        value_rows = reduced_precision(reduced_precision_back(project_rows(normalized_input, value_matrix))).reshape(SEQUENCE_COUNT, SEQUENCE_LENGTH, KEY_VALUE_HEADS, HEAD_SIZE)
        mixed = lax.map(jax.checkpoint(attend_whole), (query_matrix, key_rows, value_rows))
        mixed = reduced_precision(reduced_precision_back(mixed))
        hidden = tokens + reduced_precision_back(project_rows(mixed, out_w))
        normed_ffn = reduced_precision(rms_norm(hidden, second_gain))
        gate = reduced_precision_back(project_rows(normed_ffn, gate_w))
        up_part = reduced_precision_back(project_rows(normed_ffn, up_w))
        act = reduced_precision(jax.nn.silu(gate) * up_part)
        return hidden + project_rows(act, down_w)
    natural_inputs = to_natural(inputs).astype(jnp.float32)
    result, pullback = jax.vjp(forward, natural_inputs, attn_gain.astype(jnp.float32), query_weight.astype(jnp.float32), key_projection_weight.astype(jnp.float32), value_projection_weight.astype(jnp.float32), out_weight.astype(jnp.float32), ffn_gain.astype(jnp.float32), gate_weight.astype(jnp.float32), up_weight.astype(jnp.float32), down_weight.astype(jnp.float32))
    grads = pullback(to_natural(cotangent).astype(jnp.float32))
    return (to_pairs(result).astype(jnp.bfloat16), to_pairs(grads[0]), grads[1], grads[2], grads[3], grads[4], grads[5], grads[6], grads[7], grads[8], grads[9])
```

```python
import functools

import jax
import jax.numpy as jnp
from jax import lax
from jax.experimental import pallas as pl
from jax.experimental.pallas import tpu as pltpu
from jax.sharding import PartitionSpec as P

QUERY_HEADS = 15
KEY_VALUE_HEADS = 5
HEAD_SIZE = 64
GROUP = QUERY_HEADS // KEY_VALUE_HEADS
KV = KEY_VALUE_HEADS * HEAD_SIZE
SCALE = HEAD_SIZE**-0.5
VMEM = 50 * 1024 * 1024

eps = 1e-05
theta_base = 100000.0
bf16, f32 = jnp.bfloat16, jnp.float32


def dot(left, right, contract=((1,), (0,))):
    return lax.dot_general(left, right, (contract, ((), ())), preferred_element_type=f32)


NT = ((1,), (1,))
TN = ((0,), (0,))


def query_quarter(half, member, quarters):
    return jnp.where(half == 0, member, quarters - 1 - member)


def split_heads(source, target, half_rows):
    for half in range(2):
        rows = slice(half * half_rows, (half + 1) * half_rows)
        for g in range(KEY_VALUE_HEADS):
            for i in range(GROUP):
                lane = (g * GROUP + i) * HEAD_SIZE
                yield half, g, slice(i * half_rows, (i + 1) * half_rows), rows, slice(
                    lane, lane + HEAD_SIZE
                )


def diagonal_mask(tq):
    key_at = lax.broadcasted_iota(jnp.int32, (tq, GROUP * tq), 0)
    query_at = lax.broadcasted_iota(jnp.int32, (tq, GROUP * tq), 1) % tq
    return key_at <= query_at


def forward_kernel(member_ref, q_ref, kv_ref, mixed_ref, lse_ref, qh, top_s, sum_s, acc_s):
    tq = q_ref.shape[0] // 2
    quarters = kv_ref.shape[0] // tq
    member = member_ref[0]
    for half, g, hr, rows, lanes in split_heads(q_ref, qh, tq):
        qh[half, g, hr, :] = q_ref[rows, lanes] * jnp.asarray(SCALE, bf16)

    def one_half(half, _):
        own = query_quarter(half, member, quarters)

        def tile(ki, first):
            rows = pl.ds(pl.multiple_of(ki * tq, tq), tq)
            for g in range(KEY_VALUE_HEADS):
                keys = kv_ref[rows, g * HEAD_SIZE : (g + 1) * HEAD_SIZE]
                values = kv_ref[rows, KV + g * HEAD_SIZE : KV + (g + 1) * HEAD_SIZE]
                scores = dot(keys, qh[half, g], NT)
                if first:
                    scores = jnp.where(diagonal_mask(tq), scores, -1e30)
                    top = jnp.max(scores, axis=0, keepdims=True)
                    weights = jnp.exp(scores - top)
                    sum_s[g] = jnp.sum(weights, axis=0, keepdims=True)
                    acc_s[g] = dot(values, weights.astype(bf16), TN)
                else:
                    before = top_s[g]
                    top = jnp.maximum(before, jnp.max(scores, axis=0, keepdims=True))
                    weights = jnp.exp(scores - top)
                    fade = jnp.exp(before - top)
                    sum_s[g] = sum_s[g] * fade + jnp.sum(weights, axis=0, keepdims=True)
                    acc_s[g] = acc_s[g] * fade + dot(values, weights.astype(bf16), TN)
                top_s[g] = top

        tile(own, True)

        def body(ki, _):
            tile(ki, False)
            return 0

        lax.fori_loop(0, own, body, 0)
        rows = pl.ds(pl.multiple_of(half * tq, tq), tq)
        for g in range(KEY_VALUE_HEADS):
            total = sum_s[g]
            mixed = (acc_s[g] / total).T
            lse_ref[half, g] = top_s[g] + jnp.log(total)
            for i in range(GROUP):
                lane = (g * GROUP + i) * HEAD_SIZE
                mixed_ref[rows, lane : lane + HEAD_SIZE] = mixed[i * tq : (i + 1) * tq].astype(bf16)
        return 0

    lax.fori_loop(0, 2, one_half, 0)


def attention_forward(member, query, kv):
    rows, width = query.shape
    tq = rows // 2
    vm = pl.BlockSpec(memory_space=pltpu.VMEM)
    row = (KEY_VALUE_HEADS, 1, GROUP * tq)
    flops = 4 * 5 * tq * tq * width
    return pl.pallas_call(
        forward_kernel,
        out_shape=(
            jax.ShapeDtypeStruct((rows, width), bf16),
            jax.ShapeDtypeStruct((2,) + row, f32),
        ),
        in_specs=[pl.BlockSpec(memory_space=pltpu.SMEM), vm, vm],
        out_specs=(vm, vm),
        scratch_shapes=[
            pltpu.VMEM((2, KEY_VALUE_HEADS, GROUP * tq, HEAD_SIZE), bf16),
            pltpu.VMEM(row, f32),
            pltpu.VMEM(row, f32),
            pltpu.VMEM((KEY_VALUE_HEADS, HEAD_SIZE, GROUP * tq), f32),
        ],
        compiler_params=pltpu.CompilerParams(vmem_limit_bytes=VMEM),
        cost_estimate=pl.CostEstimate(
            flops=flops * 8, bytes_accessed=4 * rows * width, transcendentals=flops // 256
        ),
        name="attention_forward",
    )(member, query, kv)


def backward_kernel(
    member_ref, q_ref, kv_ref, mixed_ref, grad_ref, lse_ref, dq_ref, dkv_ref, qh, gh, delta, dq_s, dk_s, dv_s
):
    tq = q_ref.shape[0] // 2
    quarters = kv_ref.shape[0] // tq
    member = member_ref[0]
    ones = jnp.ones((8, HEAD_SIZE), bf16)
    for half, g, hr, rows, lanes in split_heads(q_ref, qh, tq):
        qh[half, g, hr, :] = q_ref[rows, lanes] * jnp.asarray(SCALE, bf16)
        grads = grad_ref[rows, lanes]
        gh[half, g, hr, :] = grads
        product = grads.astype(f32) * mixed_ref[rows, lanes].astype(f32)
        high = product.astype(bf16)
        low = (product - high.astype(f32)).astype(bf16)
        delta[half, g, :, hr] = (dot(ones, high, NT) + dot(ones, low, NT))[0:1]
    dk_s[...] = jnp.zeros_like(dk_s)
    dv_s[...] = jnp.zeros_like(dv_s)

    def one_half(half, _):
        own = query_quarter(half, member, quarters)

        def tile(ki, first):
            rows = pl.ds(pl.multiple_of(ki * tq, tq), tq)
            for g in range(KEY_VALUE_HEADS):
                keys = kv_ref[rows, g * HEAD_SIZE : (g + 1) * HEAD_SIZE]
                values = kv_ref[rows, KV + g * HEAD_SIZE : KV + (g + 1) * HEAD_SIZE]
                query = qh[half, g]
                grads = gh[half, g]
                probs = jnp.exp(dot(keys, query, NT) - lse_ref[half, g])
                if first:
                    probs = jnp.where(diagonal_mask(tq), probs, 0.0)
                grad_probs = dot(values, grads, NT)
                dv_s[g, rows, :] += dot(probs.astype(bf16), grads)
                grad_scores = (probs * (grad_probs - delta[half, g])).astype(bf16)
                dk_s[g, rows, :] += dot(grad_scores, query)
                dq = dot(keys, grad_scores, TN)
                if first:
                    dq_s[g] = dq
                else:
                    dq_s[g] += dq

        tile(own, True)

        def body(ki, _):
            tile(ki, False)
            return 0

        lax.fori_loop(0, own, body, 0)
        rows = pl.ds(pl.multiple_of(half * tq, tq), tq)
        for g in range(KEY_VALUE_HEADS):
            dq = (dq_s[g] * SCALE).T
            for i in range(GROUP):
                lane = (g * GROUP + i) * HEAD_SIZE
                dq_ref[rows, lane : lane + HEAD_SIZE] = dq[i * tq : (i + 1) * tq]
        return 0

    lax.fori_loop(0, 2, one_half, 0)
    for g in range(KEY_VALUE_HEADS):
        dkv_ref[:, g * HEAD_SIZE : (g + 1) * HEAD_SIZE] = dk_s[g]
        dkv_ref[:, KV + g * HEAD_SIZE : KV + (g + 1) * HEAD_SIZE] = dv_s[g]


def attention_backward(member, query, kv, mixed, grad_mixed, lse):
    rows, width = query.shape
    tq = rows // 2
    vm = pl.BlockSpec(memory_space=pltpu.VMEM)
    heads = (2, KEY_VALUE_HEADS, GROUP * tq, HEAD_SIZE)
    flops = 10 * 5 * tq * tq * width
    return pl.pallas_call(
        backward_kernel,
        out_shape=(
            jax.ShapeDtypeStruct((rows, width), f32),
            jax.ShapeDtypeStruct(kv.shape, f32),
        ),
        in_specs=[pl.BlockSpec(memory_space=pltpu.SMEM)] + [vm] * 5,
        out_specs=(vm, vm),
        scratch_shapes=[
            pltpu.VMEM(heads, bf16),
            pltpu.VMEM(heads, bf16),
            pltpu.VMEM((2, KEY_VALUE_HEADS, 1, GROUP * tq), f32),
            pltpu.VMEM((KEY_VALUE_HEADS, HEAD_SIZE, GROUP * tq), f32),
            pltpu.VMEM((KEY_VALUE_HEADS, kv.shape[0], HEAD_SIZE), f32),
            pltpu.VMEM((KEY_VALUE_HEADS, kv.shape[0], HEAD_SIZE), f32),
        ],
        compiler_params=pltpu.CompilerParams(vmem_limit_bytes=VMEM),
        cost_estimate=pl.CostEstimate(
            flops=flops * 8, bytes_accessed=12 * rows * width, transcendentals=flops // 640
        ),
        name="attention_backward",
    )(member, query, kv, mixed, grad_mixed, lse)


def rope_tables(positions):
    half = HEAD_SIZE // 2
    freqs = theta_base ** (-jnp.arange(half, dtype=f32) * 2.0 / HEAD_SIZE)
    angles = positions[:, None] * freqs
    cosine, sine = jnp.cos(angles), jnp.sin(angles)
    return jnp.concatenate([cosine, cosine], axis=1), jnp.concatenate([sine, sine], axis=1)


def rotate(rows):
    half = HEAD_SIZE // 2
    width = rows.shape[1]
    ahead = jnp.concatenate([rows[:, half:], rows[:, :half]], axis=1)
    behind = jnp.concatenate([rows[:, width - half :], rows[:, : width - half]], axis=1)
    lane = lax.broadcasted_iota(jnp.int32, rows.shape, 1) % HEAD_SIZE
    return jnp.where(lane < half, -ahead, behind)


def widen(table, width):
    return jnp.concatenate([table] * (width // HEAD_SIZE), axis=1)


def rotate_pairs(rows, cosine, sine):
    width = rows.shape[1]
    return rows * widen(cosine, width) + rotate(rows) * widen(sine, width)


def rotate_pairs_back(grads, cosine, sine):
    width = grads.shape[1]
    return grads * widen(cosine, width) - rotate(grads * widen(sine, width))


def norm_forward(rows, gain):
    inverse = lax.rsqrt(jnp.mean(rows * rows, axis=-1, keepdims=True) + eps)
    return rows * inverse * gain, inverse


def norm_backward(rows, inverse, gain, grad_normed):
    scaled = grad_normed * gain
    gain_grad = jnp.sum(grad_normed * rows * inverse, axis=0)
    value_grad = inverse * scaled - rows * inverse**3 * jnp.mean(
        scaled * rows, axis=-1, keepdims=True
    )
    return value_grad, gain_grad


class Layout:
    def __init__(self, seqs):
        self.S = seqs
        self.Pn = lax.axis_size("ctx")
        self.F = lax.axis_size("fsdp")
        self.places = self.Pn // (2 * seqs)
        self.G = 2 * self.places
        self.t = lax.axis_index("ctx")
        self.f = lax.axis_index("fsdp")
        core = self.f % 2
        self.member = (self.t % self.places) * 2 + core
        self.sequence = (self.t // self.places) % seqs

    def spread(self, r):
        pairs = []
        for u in range(self.Pn):
            for f in range(self.F):
                s = (u % self.S + r) % self.S
                m = u // self.S
                t = ((f % 2) * self.S + s) * self.places + m // 2
                pairs.append((u * self.F + f, t * self.F + (f // 2) * 2 + m % 2))
        return pairs

    def ring(self, r):
        pairs = []
        for t in range(self.Pn):
            for f in range(self.F):
                base = t - t % self.places
                m = ((t % self.places) * 2 + f % 2 + r) % self.G
                pairs.append((t * self.F + f, (base + m // 2) * self.F + (f // 2) * 2 + m % 2))
        return pairs

    def to_sequence(self, array):
        got = []
        for r in range(self.S):
            piece = lax.dynamic_index_in_dim(
                array, (self.t % self.S + r) % self.S, 0, keepdims=False
            )
            got.append(lax.ppermute(piece, ("ctx", "fsdp"), self.spread(r)))
        ordered = jnp.stack(got[::-1] + got[::-1])
        start = (self.S - 1 - self.sequence) % self.S
        ordered = lax.dynamic_slice_in_dim(ordered, start, self.S, 0)
        low, high = ordered[:, 0], ordered[::-1, 1]
        block, width = array.shape[2], array.shape[3]
        return jnp.concatenate(
            [low.reshape(self.S * block, width), high.reshape(self.S * block, width)], axis=0
        )

    def from_sequence(self, rows):
        width = rows.shape[1]
        block = rows.shape[0] // (2 * self.S)
        halves = rows.reshape(2, self.S, block, width)
        array = jnp.stack([halves[0], halves[1, ::-1]], axis=1)
        got = []
        for r in range(self.S):
            piece = lax.dynamic_index_in_dim(
                array, (self.sequence - r + self.S) % self.S, 0, keepdims=False
            )
            back = [(b, a) for a, b in self.spread(r)]
            got.append(lax.ppermute(piece, ("ctx", "fsdp"), back))
        ordered = jnp.stack(got + got)
        start = (self.S - self.t % self.S) % self.S
        return lax.dynamic_slice_in_dim(ordered, start, self.S, 0)

    def gather_group(self, rows):
        tq, width = rows.shape[0] // 2, rows.shape[1]
        got = [rows] + [
            lax.ppermute(rows, ("ctx", "fsdp"), self.ring(r)) for r in range(1, self.G)
        ]
        got = [g.reshape(2, tq, width) for g in got]
        if self.G == 2:
            even = self.member == 0
            first, second = jnp.where(even, got[0], got[1]), jnp.where(even, got[1], got[0])
            whole = jnp.stack([first[0], second[0], second[1], first[1]])
        else:
            ordered = jnp.stack(got[::-1] + got[::-1])
            ordered = lax.dynamic_slice_in_dim(ordered, (self.G - 1 - self.member), self.G, 0)
            whole = jnp.concatenate([ordered[:, 0], ordered[::-1, 1]])
        return whole.reshape(2 * self.G * tq, width)

    def scatter_group(self, rows):
        quarters = 2 * self.G
        tq, width = rows.shape[0] // quarters, rows.shape[1]
        parts = rows.reshape(quarters, tq, width)

        def of(m):
            low = lax.dynamic_index_in_dim(parts, m, 0, keepdims=False)
            high = lax.dynamic_index_in_dim(parts, quarters - 1 - m, 0, keepdims=False)
            return jnp.concatenate([low, high])

        total = of(self.member)
        for r in range(1, self.G):
            piece = of((self.member + r) % self.G).astype(bf16)
            total = total + lax.ppermute(piece, ("ctx", "fsdp"), self.ring(r)).astype(f32)
        return total


def swap(array, axis, bit):
    size = lax.axis_size(axis)
    return lax.ppermute(array, axis, [(i, i ^ bit) for i in range(size)])


def choose(flag, one, other):
    return jnp.where(flag, one, other)


def gather_halves(low, high):
    f, y = lax.axis_index("fsdp"), lax.axis_index("ctx") % 2
    crossed = swap(choose(y == 0, low, high), "fsdp", 2)
    passed = swap(crossed, "ctx", 1)
    far_low, far_high = choose(y == 0, crossed, passed), choose(y == 0, passed, crossed)
    out = []
    for near, far in ((low, far_low), (high, far_high)):
        other = swap(jnp.stack([near, far]), "fsdp", 1)
        rows = near.shape[0]
        full = jnp.zeros((4 * rows, near.shape[1]), near.dtype)
        for piece, place in ((near, f), (far, f ^ 2), (other[0], f ^ 1), (other[1], f ^ 3)):
            full = lax.dynamic_update_slice_in_dim(full, piece, place * rows, 0)
        out.append(full)
    return out


def scatter_sum(grads, cols):
    f, t = lax.axis_index("fsdp"), lax.axis_index("ctx")
    rows = grads.shape[0] // 4
    core, x, y, z = f % 2, f // 2, t % 2, t // 2

    def add(one, other):
        return (one.astype(f32) + other.astype(f32)).astype(bf16)

    parts = grads.reshape(2, 2, rows, grads.shape[1])
    even, odd = parts[:, 0], parts[:, 1]
    both = add(choose(core == 0, even, odd), swap(choose(core == 0, odd, even), "fsdp", 1))
    half = add(choose(x == 0, both[0], both[1]), swap(choose(x == 0, both[1], both[0]), "fsdp", 2))
    places = [half[:, i * cols : (i + 1) * cols] for i in range(8)]
    even, odd = jnp.stack(places[0::2]), jnp.stack(places[1::2])
    line = add(choose(y == 0, even, odd), swap(choose(y == 0, odd, even), "ctx", 1))

    def own(k):
        return lax.dynamic_index_in_dim(line, jnp.clip(k, 0, 3), 0, keepdims=False)

    up = down = None
    for step in range(1, 4):
        send_up, send_down = own(z + 4 - step), own(z - 4 + step)
        if step > 1:
            send_up, send_down = add(send_up, up), add(send_down, down)
        ups = [(2 * k + j, 2 * k + 2 + j) for k in range(step) for j in range(2)]
        downs = [(2 * (3 - k) + j, 2 * (3 - k) - 2 + j) for k in range(step) for j in range(2)]
        up, down = lax.ppermute(send_up, "ctx", ups), lax.ppermute(send_down, "ctx", downs)
    return own(z).astype(f32) + up.astype(f32) + down.astype(f32)


def shards(
    inputs,
    attn_gain,
    query_weight,
    key_projection_weight,
    value_projection_weight,
    out_weight,
    ffn_gain,
    gate_weight,
    up_weight,
    down_weight,
    positions,
    cotangent,
):
    seqs, _, _, block, width = inputs.shape
    lay = Layout(seqs)
    fast = lay.F == 4 and lay.Pn == 8
    ff = gate_weight.shape[1]

    place = positions.reshape(seqs, 2, block, 1)
    packed = jnp.concatenate(
        [
            inputs.reshape(seqs, 2, block, width),
            (place // 128).astype(bf16),
            (place % 128).astype(bf16),
        ],
        axis=-1,
    )
    packed = lay.to_sequence(packed)
    residual = packed[:, :width].astype(f32)
    place = packed[:, width].astype(f32) * 128.0 + packed[:, width + 1].astype(f32)
    member = lay.member.astype(jnp.int32).reshape(1)

    gains = lax.all_gather(jnp.stack([attn_gain, ffn_gain]), "fsdp", axis=1, tiled=True)
    gains = gains.astype(f32)
    first_gain, second_gain = gains[0], gains[1]
    if fast:
        attn_low = jnp.concatenate([query_weight, key_projection_weight], axis=1)
        attn_high = jnp.concatenate([value_projection_weight, out_weight], axis=1)
        low, high = gather_halves(attn_low, attn_high)
        query_full, key_full = low[:, :width], low[:, width:]
        value_full, out_full = high[:, :KV], high[:, KV:]
        gate_full, up_full = gather_halves(gate_weight, up_weight)
        rows = down_weight.shape[0] // 2
        down_low, down_high = gather_halves(down_weight[:rows], down_weight[rows:])
        down_full = jnp.stack(
            [down_low.reshape(4, rows, width), down_high.reshape(4, rows, width)], axis=1
        ).reshape(ff, width)
    else:
        query_full, key_full, value_full, out_full, gate_full, up_full, down_full = [
            lax.all_gather(w, "fsdp", axis=0, tiled=True)
            for w in (
                query_weight,
                key_projection_weight,
                value_projection_weight,
                out_weight,
                gate_weight,
                up_weight,
                down_weight,
            )
        ]

    cosine, sine = rope_tables(place)
    normalized, inverse_first = norm_forward(residual, first_gain)
    normed = normalized.astype(bf16)
    query = rotate_pairs(dot(normed, query_full), cosine, sine).astype(bf16)
    keys = rotate_pairs(dot(normed, key_full), cosine, sine).astype(bf16)
    values = dot(normed, value_full).astype(bf16)
    kv = lay.gather_group(jnp.concatenate([keys, values], axis=1))
    mixed, lse = attention_forward(member, query, kv)
    hidden = residual + dot(mixed, out_full)

    grad_rows = lay.to_sequence(cotangent.reshape(seqs, 2, block, width))
    normed_ffn, inverse_second = norm_forward(hidden, second_gain)
    normed_ffn = normed_ffn.astype(bf16)
    gate = dot(normed_ffn, gate_full)
    up_part = dot(normed_ffn, up_full)
    sigmoid = jax.nn.sigmoid(gate)
    act = (gate * sigmoid * up_part).astype(bf16)
    outputs = lay.from_sequence((hidden + dot(act, down_full)).astype(bf16))
    down_grad = dot(act, grad_rows, TN).astype(bf16)
    grad_act = dot(grad_rows, down_full, NT)
    grad_up = (grad_act * gate * sigmoid).astype(bf16)
    grad_gate = (grad_act * up_part * sigmoid * (1.0 + gate * (1.0 - sigmoid))).astype(bf16)
    gate_grad = dot(normed_ffn, grad_gate, TN).astype(bf16)
    up_grad = dot(normed_ffn, grad_up, TN).astype(bf16)
    grad_normed_ffn = dot(grad_gate, gate_full, NT) + dot(grad_up, up_full, NT)
    through, ffn_gain_grad = norm_backward(hidden, inverse_second, second_gain, grad_normed_ffn)
    grad_hidden = grad_rows.astype(f32) + through
    grad_branch = grad_hidden.astype(bf16)
    out_grad = dot(mixed, grad_branch, TN).astype(bf16)
    grad_mixed = dot(grad_branch, out_full, NT).astype(bf16)

    dq, dkv = attention_backward(member, query, kv, mixed, grad_mixed, lse)
    dkv = lay.scatter_group(dkv)
    grad_query = rotate_pairs_back(dq, cosine, sine).astype(bf16)
    grad_key = rotate_pairs_back(dkv[:, :KV], cosine, sine).astype(bf16)
    grad_value = dkv[:, KV:].astype(bf16)
    query_grad = dot(normed, grad_query, TN).astype(bf16)
    key_grad = dot(normed, grad_key, TN).astype(bf16)
    value_grad = dot(normed, grad_value, TN).astype(bf16)
    grad_normed = (
        dot(grad_query, query_full, NT) + dot(grad_key, key_full, NT) + dot(grad_value, value_full, NT)
    )
    grad_input, attn_gain_grad = norm_backward(residual, inverse_first, first_gain, grad_normed)
    input_grad = lay.from_sequence((grad_hidden + grad_input).astype(bf16)).astype(f32)

    def scatter(grads):
        cols = grads.shape[1] // lay.Pn
        if fast:
            return scatter_sum(grads, cols)
        part = lax.psum_scatter(grads, "fsdp", scatter_dimension=0, tiled=True)
        return lax.psum_scatter(part, "ctx", scatter_dimension=1, tiled=True).astype(f32)

    down_grad, gate_grad, up_grad, out_grad, query_grad, key_grad, value_grad = [
        scatter(g)
        for g in (down_grad, gate_grad, up_grad, out_grad, query_grad, key_grad, value_grad)
    ]
    gain_grads = lax.psum(jnp.stack([attn_gain_grad, ffn_gain_grad]), ("ctx", "fsdp"))
    gain_rows = attn_gain.shape[0]
    gain_grads = lax.dynamic_slice_in_dim(gain_grads, lay.f * gain_rows, gain_rows, 1)
    return (
        outputs.reshape(inputs.shape),
        input_grad.reshape(inputs.shape),
        gain_grads[0],
        query_grad,
        key_grad,
        value_grad,
        out_grad,
        gain_grads[1],
        gate_grad,
        up_grad,
        down_grad,
    )


def solution(mesh):
    in_specs = (
        P("fsdp", "ctx", None, None, None),
        P("fsdp"),
        P("fsdp", None),
        P("fsdp", None),
        P("fsdp", None),
        P("fsdp", None),
        P("fsdp"),
        P("fsdp", None),
        P("fsdp", None),
        P("fsdp", None),
        P("fsdp", "ctx", None, None),
        P("fsdp", "ctx", None, None, None),
    )
    out_specs = (
        P("fsdp", "ctx", None, None, None),
        P("fsdp", "ctx", None, None, None),
        P("fsdp"),
        P("fsdp", "ctx"),
        P("fsdp", "ctx"),
        P("fsdp", "ctx"),
        P("fsdp", "ctx"),
        P("fsdp"),
        P("fsdp", "ctx"),
        P("fsdp", "ctx"),
        P("fsdp", "ctx"),
    )
    return jax.shard_map(shards, mesh=mesh, in_specs=in_specs, out_specs=out_specs, check_vma=False)
```

```python
import functools
import math

import jax
import jax.numpy as jnp
from jax import lax
from jax.experimental import pallas as pl
from jax.experimental.pallas import tpu as pltpu
from jax.sharding import PartitionSpec as P

QUERY_HEADS = 15
KEY_VALUE_HEADS = 5
HEAD_SIZE = 64
GROUP = QUERY_HEADS // KEY_VALUE_HEADS
KV = KEY_VALUE_HEADS * HEAD_SIZE
SCALE = HEAD_SIZE**-0.5
VMEM = 50 * 1024 * 1024

eps = 1e-05
theta_base = 100000.0
bf16, f32 = jnp.bfloat16, jnp.float32


def dot(left, right, contract=((1,), (0,))):
    return lax.dot_general(left, right, (contract, ((), ())), preferred_element_type=f32)


NT = ((1,), (1,))
TN = ((0,), (0,))


def query_quarter(half, member, quarters):
    return jnp.where(half == 0, member, quarters - 1 - member)


def split_heads(source, target, half_rows):
    for half in range(2):
        rows = slice(half * half_rows, (half + 1) * half_rows)
        for g in range(KEY_VALUE_HEADS):
            for i in range(GROUP):
                lane = (g * GROUP + i) * HEAD_SIZE
                yield half, g, slice(i * half_rows, (i + 1) * half_rows), rows, slice(
                    lane, lane + HEAD_SIZE
                )


def diagonal_mask(tq):
    key_at = lax.broadcasted_iota(jnp.int32, (tq, GROUP * tq), 0)
    query_at = lax.broadcasted_iota(jnp.int32, (tq, GROUP * tq), 1) % tq
    return key_at <= query_at


def place_pieces(member, pieces, target, tq):
    quarters = target.shape[0] // tq
    group = quarters // 2
    for r, piece in enumerate(pieces):
        m = lax.rem(member + group - r, group)
        target[pl.ds(pl.multiple_of(m * tq, tq), tq), :] = piece[0:tq, :]
        high = pl.multiple_of((quarters - 1 - m) * tq, tq)
        target[pl.ds(high, tq), :] = piece[tq : 2 * tq, :]


def forward_kernel(group, member_ref, q_ref, *refs):
    pieces, refs = refs[:group], refs[group:]
    mixed_ref, mixed_t_ref, lse_ref, kv_ref, qh, top_s, sum_s, acc_s = refs
    tq = q_ref.shape[0] // 2
    quarters = 2 * group
    member = member_ref[0]
    place_pieces(member, pieces, kv_ref, tq)
    for half, g, hr, rows, lanes in split_heads(q_ref, qh, tq):
        qh[half, g, hr, :] = q_ref[rows, lanes] * jnp.asarray(SCALE, bf16)

    def one_half(half, _):
        own = query_quarter(half, member, quarters)

        def tile(ki, first):
            rows = pl.ds(pl.multiple_of(ki * tq, tq), tq)
            for g in range(KEY_VALUE_HEADS):
                keys = kv_ref[rows, g * HEAD_SIZE : (g + 1) * HEAD_SIZE]
                values = kv_ref[rows, KV + g * HEAD_SIZE : KV + (g + 1) * HEAD_SIZE]
                scores = dot(keys, qh[half, g], NT)
                if first:
                    scores = jnp.where(diagonal_mask(tq), scores, -1e30)
                    top = jnp.max(scores, axis=0, keepdims=True)
                    weights = jnp.exp(scores - top)
                    sum_s[g] = jnp.sum(weights, axis=0, keepdims=True)
                    acc_s[g] = dot(values, weights.astype(bf16), TN)
                else:
                    before = top_s[g]
                    top = jnp.maximum(before, jnp.max(scores, axis=0, keepdims=True))
                    weights = jnp.exp(scores - top)
                    fade = jnp.exp(before - top)
                    sum_s[g] = sum_s[g] * fade + jnp.sum(weights, axis=0, keepdims=True)
                    acc_s[g] = acc_s[g] * fade + dot(values, weights.astype(bf16), TN)
                top_s[g] = top

        tile(own, True)

        def body(ki, _):
            tile(ki, False)
            return 0

        lax.fori_loop(0, own, body, 0)
        rows = pl.ds(pl.multiple_of(half * tq, tq), tq)
        for g in range(KEY_VALUE_HEADS):
            total = sum_s[g]
            mixed_t = acc_s[g] / total
            mixed = mixed_t.T
            lse_ref[half, g] = top_s[g] + jnp.log(total)
            for i in range(GROUP):
                lane = (g * GROUP + i) * HEAD_SIZE
                here = slice(i * tq, (i + 1) * tq)
                mixed_ref[rows, lane : lane + HEAD_SIZE] = mixed[here].astype(bf16)
                mixed_t_ref[lane : lane + HEAD_SIZE, rows] = mixed_t[:, here].astype(bf16)
        return 0

    lax.fori_loop(0, 2, one_half, 0)


VM = pl.BlockSpec(memory_space=pltpu.VMEM)
SM = pl.BlockSpec(memory_space=pltpu.SMEM)
ANY = pl.BlockSpec(memory_space=pl.ANY)


def call(kernel, name, outs, ins, specs, scratch, flops, special=0, far=()):
    moved = sum(i.size * i.dtype.itemsize for i in ins)
    moved += sum(o.size * o.dtype.itemsize for o in outs)
    return pl.pallas_call(
        kernel,
        out_shape=tuple(outs),
        in_specs=specs,
        out_specs=tuple(ANY if i in far else VM for i in range(len(outs))),
        scratch_shapes=scratch,
        compiler_params=pltpu.CompilerParams(vmem_limit_bytes=VMEM),
        cost_estimate=pl.CostEstimate(
            flops=int(flops), bytes_accessed=int(moved), transcendentals=int(special)
        ),
        name=name,
    )(*ins)


def shaped(dims, kind):
    return jax.ShapeDtypeStruct(dims, kind)


def attention_forward(member, query, pieces):
    rows, width = query.shape
    tq, group = rows // 2, len(pieces)
    row = (KEY_VALUE_HEADS, 1, GROUP * tq)
    return call(
        functools.partial(forward_kernel, group),
        "attention_forward",
        [shaped((rows, width), bf16), shaped((width, rows), bf16), shaped((2,) + row, f32)],
        [member, query, *pieces],
        [SM] + [VM] * (1 + group),
        [
            pltpu.VMEM((2 * group * tq, 2 * KV), bf16),
            pltpu.VMEM((2, KEY_VALUE_HEADS, GROUP * tq, HEAD_SIZE), bf16),
            pltpu.VMEM(row, f32),
            pltpu.VMEM(row, f32),
            pltpu.VMEM((KEY_VALUE_HEADS, HEAD_SIZE, GROUP * tq), f32),
        ],
        8e9,
        4e6,
    )


def backward_kernel(group, member_ref, q_ref, *refs):
    pieces, refs = refs[:group], refs[group:]
    (mixed_ref, grad_ref, lse_ref, dq_ref, own_ref), refs = refs[:5], refs[5:]
    send_refs, refs = refs[: group - 1], refs[group - 1 :]
    kv_ref, qh, gh, delta, dq_s, dk_s, dv_s = refs
    tq = q_ref.shape[0] // 2
    quarters = 2 * group
    member = member_ref[0]
    place_pieces(member, pieces, kv_ref, tq)
    ones = jnp.ones((8, HEAD_SIZE), bf16)
    for half, g, hr, rows, lanes in split_heads(q_ref, qh, tq):
        qh[half, g, hr, :] = q_ref[rows, lanes] * jnp.asarray(SCALE, bf16)
        grads = grad_ref[rows, lanes]
        gh[half, g, hr, :] = grads
        product = grads.astype(f32) * mixed_ref[rows, lanes].astype(f32)
        high = product.astype(bf16)
        low = (product - high.astype(f32)).astype(bf16)
        delta[half, g, :, hr] = (dot(ones, high, NT) + dot(ones, low, NT))[0:1]
    dk_s[...] = jnp.zeros_like(dk_s)
    dv_s[...] = jnp.zeros_like(dv_s)

    def one_half(half, _):
        own = query_quarter(half, member, quarters)

        def tile(ki, first):
            rows = pl.ds(pl.multiple_of(ki * tq, tq), tq)
            for g in range(KEY_VALUE_HEADS):
                keys = kv_ref[rows, g * HEAD_SIZE : (g + 1) * HEAD_SIZE]
                values = kv_ref[rows, KV + g * HEAD_SIZE : KV + (g + 1) * HEAD_SIZE]
                query = qh[half, g]
                grads = gh[half, g]
                probs = jnp.exp(dot(keys, query, NT) - lse_ref[half, g])
                if first:
                    probs = jnp.where(diagonal_mask(tq), probs, 0.0)
                grad_probs = dot(values, grads, NT)
                dv_s[g, rows, :] += dot(probs.astype(bf16), grads)
                grad_scores = (probs * (grad_probs - delta[half, g])).astype(bf16)
                dk_s[g, rows, :] += dot(grad_scores, query)
                dq = dot(keys, grad_scores, TN)
                if first:
                    dq_s[g] = dq
                else:
                    dq_s[g] += dq

        tile(own, True)

        def body(ki, _):
            tile(ki, False)
            return 0

        lax.fori_loop(0, own, body, 0)
        rows = pl.ds(pl.multiple_of(half * tq, tq), tq)
        for g in range(KEY_VALUE_HEADS):
            dq = (dq_s[g] * SCALE).T
            for i in range(GROUP):
                lane = (g * GROUP + i) * HEAD_SIZE
                dq_ref[rows, lane : lane + HEAD_SIZE] = dq[i * tq : (i + 1) * tq]
        return 0

    lax.fori_loop(0, 2, one_half, 0)
    for r, target in enumerate((own_ref,) + tuple(send_refs)):
        m = lax.rem(member + r, group)
        for part, quarter in ((0, m), (1, quarters - 1 - m)):
            rows = pl.ds(pl.multiple_of(quarter * tq, tq), tq)
            there = slice(part * tq, (part + 1) * tq)
            for g in range(KEY_VALUE_HEADS):
                lane = g * HEAD_SIZE
                target[there, lane : lane + HEAD_SIZE] = dk_s[g, rows, :].astype(target.dtype)
                lane = KV + g * HEAD_SIZE
                target[there, lane : lane + HEAD_SIZE] = dv_s[g, rows, :].astype(target.dtype)


def attention_backward(member, query, pieces, mixed, grad_mixed, lse):
    rows, width = query.shape
    tq, group = rows // 2, len(pieces)
    heads = (2, KEY_VALUE_HEADS, GROUP * tq, HEAD_SIZE)
    total = 2 * group * tq
    outs = [shaped((rows, width), f32), shaped((rows, 2 * KV), f32)]
    return call(
        functools.partial(backward_kernel, group),
        "attention_backward",
        outs + [shaped((rows, 2 * KV), bf16)] * (group - 1),
        [member, query, *pieces, mixed, grad_mixed, lse],
        [SM] + [VM] * (4 + group),
        [
            pltpu.VMEM((total, 2 * KV), bf16),
            pltpu.VMEM(heads, bf16),
            pltpu.VMEM(heads, bf16),
            pltpu.VMEM((2, KEY_VALUE_HEADS, 1, GROUP * tq), f32),
            pltpu.VMEM((KEY_VALUE_HEADS, HEAD_SIZE, GROUP * tq), f32),
            pltpu.VMEM((KEY_VALUE_HEADS, total, HEAD_SIZE), f32),
            pltpu.VMEM((KEY_VALUE_HEADS, total, HEAD_SIZE), f32),
        ],
        16e9,
        4e6,
    )


def rope_tables(positions):
    half = HEAD_SIZE // 2
    freqs = theta_base ** (-jnp.arange(half, dtype=f32) * 2.0 / HEAD_SIZE)
    angles = positions[:, None] * freqs
    cosine, sine = jnp.cos(angles), jnp.sin(angles)
    return jnp.concatenate([cosine, cosine], axis=1), jnp.concatenate([sine, sine], axis=1)


def rotate(rows):
    half = HEAD_SIZE // 2
    width = rows.shape[1]
    ahead = jnp.concatenate([rows[:, half:], rows[:, :half]], axis=1)
    behind = jnp.concatenate([rows[:, width - half :], rows[:, : width - half]], axis=1)
    lane = lax.broadcasted_iota(jnp.int32, rows.shape, 1) % HEAD_SIZE
    return jnp.where(lane < half, -ahead, behind)


def widen(table, width):
    return jnp.concatenate([table] * (width // HEAD_SIZE), axis=1)


def rotate_pairs(rows, cosine, sine):
    width = rows.shape[1]
    return rows * widen(cosine, width) + rotate(rows) * widen(sine, width)


def rotate_pairs_back(grads, cosine, sine):
    width = grads.shape[1]
    return grads * widen(cosine, width) - rotate(grads * widen(sine, width))


def norm_forward(rows, gain):
    inverse = lax.rsqrt(jnp.mean(rows * rows, axis=-1, keepdims=True) + eps)
    return rows * inverse * gain, inverse


def norm_backward(rows, inverse, gain, grad_normed):
    scaled = grad_normed * gain
    gain_grad = jnp.sum(grad_normed * rows * inverse, axis=0)
    value_grad = inverse * scaled - rows * inverse**3 * jnp.mean(
        scaled * rows, axis=-1, keepdims=True
    )
    return value_grad, gain_grad


class Layout:
    def __init__(self, seqs):
        self.S = seqs
        self.Pn = lax.axis_size("ctx")
        self.F = lax.axis_size("fsdp")
        self.places = self.Pn // (2 * seqs)
        self.G = 2 * self.places
        self.t = lax.axis_index("ctx")
        self.f = lax.axis_index("fsdp")
        core = self.f % 2
        self.member = (self.t % self.places) * 2 + core
        self.sequence = (self.t // self.places) % seqs

    def spread(self, r):
        pairs = []
        for u in range(self.Pn):
            for f in range(self.F):
                s = (u % self.S + r) % self.S
                m = u // self.S
                t = ((f % 2) * self.S + s) * self.places + m // 2
                pairs.append((u * self.F + f, t * self.F + (f // 2) * 2 + m % 2))
        return pairs

    def ring(self, r):
        pairs = []
        for t in range(self.Pn):
            for f in range(self.F):
                base = t - t % self.places
                m = ((t % self.places) * 2 + f % 2 + r) % self.G
                pairs.append((t * self.F + f, (base + m // 2) * self.F + (f // 2) * 2 + m % 2))
        return pairs

    def receive(self, array):
        got = []
        for r in range(self.S):
            piece = lax.dynamic_index_in_dim(
                array, (self.t % self.S + r) % self.S, 0, keepdims=False
            )
            got.append(lax.ppermute(piece, ("ctx", "fsdp"), self.spread(r)))
        return got

    def to_sequence(self, array):
        got = self.receive(array)
        ordered = jnp.stack(got[::-1] + got[::-1])
        start = (self.S - 1 - self.sequence) % self.S
        ordered = lax.dynamic_slice_in_dim(ordered, start, self.S, 0)
        low, high = ordered[:, 0], ordered[::-1, 1]
        block, width = array.shape[2], array.shape[3]
        return jnp.concatenate(
            [low.reshape(self.S * block, width), high.reshape(self.S * block, width)], axis=0
        )

    def from_sequence(self, rows):
        return self.place_back([self.send_back(rows, r) for r in range(self.S)])

    def send_back(self, rows, r):
        width = rows.shape[1]
        block = rows.shape[0] // (2 * self.S)
        halves = rows.reshape(2, self.S, block, width)
        slot = (self.sequence - r + self.S) % self.S
        low = lax.dynamic_index_in_dim(halves[0], slot, 0, keepdims=False)
        high = lax.dynamic_index_in_dim(halves[1], self.S - 1 - slot, 0, keepdims=False)
        back = [(b, a) for a, b in self.spread(r)]
        return lax.ppermute(jnp.stack([low, high]), ("ctx", "fsdp"), back)

    def place_back(self, got):
        ordered = jnp.stack(got + got)
        start = (self.S - self.t % self.S) % self.S
        return lax.dynamic_slice_in_dim(ordered, start, self.S, 0)

    def around(self, rows, r):
        return lax.ppermute(rows, ("ctx", "fsdp"), self.ring(r))

    def gather_group(self, rows):
        return [rows] + [self.around(rows, r) for r in range(1, self.G)]

    def scatter_group(self, own, sends):
        for r, piece in enumerate(sends):
            own = own + self.around(piece, r + 1).astype(f32)
        return own


def swap(array, axis, bit):
    size = lax.axis_size(axis)
    return lax.ppermute(array, axis, [(i, i ^ bit) for i in range(size)])


def after(array, *others):
    return lax.optimization_barrier((array,) + others)[0]


def add(one, other):
    return (one.astype(f32) + other.astype(f32)).astype(bf16)


class Sums:
    def __init__(self):
        f, t = lax.axis_index("fsdp"), lax.axis_index("ctx")
        self.core, self.x, self.y, self.z = f % 2, f // 2, t % 2, t // 2

    def exchange(self, mine, theirs, axis, bit):
        return add(mine, swap(theirs, axis, bit))

    def over_x(self, parts):
        return self.halves(parts[0], parts[1], self.x, "fsdp", 2)

    def halves(self, low, high, bit, axis, shift):
        flag = bit == 0
        return self.exchange(
            jnp.where(flag, low, high), jnp.where(flag, high, low), axis, shift
        )

    def lanes(self, parts, bit, axis, shift):
        half = parts.shape[-1] // 2
        return self.halves(parts[..., :half], parts[..., half:], bit, axis, shift)

    def over_y(self, parts):
        return self.lanes(parts, self.y, "ctx", 1)

    def over_z(self, parts, first=0):
        n = parts.shape[0]

        def part(z):
            return lax.dynamic_index_in_dim(parts, jnp.clip(z - first, 0, n - 1), 0, keepdims=False)

        total = part(self.z).astype(f32)
        for k in range(1, 4):
            pairs = [(t, (t + 2 * k) % 8) for t in range(8)]
            pairs = [(a, b) for a, b in pairs if first <= b // 2 < first + n]
            total = total + lax.ppermute(part((self.z + k) % 4), "ctx", pairs).astype(f32)
        return total


LANES = 128
QKV = 2 * KV + QUERY_HEADS * HEAD_SIZE


def turn(rows, sine_sign):
    half = HEAD_SIZE // 2
    ahead = pltpu.roll(rows, LANES - half, 1)
    behind = pltpu.roll(rows, half, 1)
    return jnp.where(sine_sign < 0, -ahead, behind)


def sine_signs(rows):
    lane = lax.broadcasted_iota(jnp.int32, (rows, LANES), 1) % HEAD_SIZE
    return jnp.where(lane < HEAD_SIZE // 2, -1.0, 1.0)


def project_kernel(info, *refs):
    got, refs = refs[:4], refs[4:]
    pieces, refs = refs[:4], refs[4:]
    residual, normed, normed_t, query, kv, tables, gains, w, tok = refs
    f, sequence = info[0], info[1]
    slots, block = 4, got[0].shape[1]
    rows, width = residual.shape
    half = rows // 2
    for r in range(slots):
        i = lax.rem(sequence + slots - r, slots)
        tok[pl.ds(pl.multiple_of(i * block, block), block), :] = got[r][0]
        high = half + (slots - 1 - i) * block
        tok[pl.ds(pl.multiple_of(high, block), block), :] = got[r][1]
    part = pieces[0].shape[0]
    for piece, bit in zip(pieces, (0, 2, 1, 3)):
        w[pl.ds(pl.multiple_of((f ^ bit) * part, 16), part), :] = piece[:, : QKV + 64]
    gains_t = w[:, QKV - 64 : QKV + 64].astype(f32).T
    gains[...] = jnp.broadcast_to(gains_t[64:65], gains.shape)
    gains[1:2, :] = gains_t[65:66]
    x = tok[:, :width].astype(f32)
    residual[...] = x
    place = tok[:, width : width + 1].astype(f32) * 128.0 + tok[:, width + 1 : width + 2].astype(f32)
    lane = lax.broadcasted_iota(jnp.int32, (1, LANES), 1) % (HEAD_SIZE // 2)
    freqs = jnp.exp(lane.astype(f32) * (-2.0 / HEAD_SIZE * math.log(theta_base)))
    angles = place * freqs
    cosine, sine = jnp.cos(angles), jnp.sin(angles)
    tables[:, :LANES] = cosine
    tables[:, LANES:] = sine
    inverse = lax.rsqrt(jnp.mean(x * x, axis=-1, keepdims=True) + eps)
    n = x * inverse * gains[0:1, :]
    normed[...] = n.astype(bf16)
    normed_t[...] = n.T.astype(bf16)
    sign = sine_signs(rows)
    low = lax.broadcasted_iota(jnp.int32, (rows, LANES), 1) < HEAD_SIZE
    for c in range(0, QKV, 2 * LANES):
        out = dot(normed[...], w[:, c : min(c + 2 * LANES, QKV + 64)])
        for at in (c, c + LANES):
            if at >= QKV:
                continue
            tile = out[:, at - c : at - c + LANES]
            turned = tile * cosine + turn(tile, sign) * sine
            if at + LANES <= KV:
                kv[:, at : at + LANES] = turned.astype(bf16)
            elif at < KV:
                kv[:, at : at + LANES] = jnp.where(low, turned, tile).astype(bf16)
            elif at < 2 * KV:
                kv[:, at : at + LANES] = tile.astype(bf16)
            else:
                q = at - 2 * KV
                n_lanes = min(LANES, width - q)
                query[:, q : q + n_lanes] = turned[:, :n_lanes].astype(bf16)


def project(info, got, pieces, width):
    rows = 8 * got[0].shape[1]
    outs = [
        shaped((rows, width), f32),
        shaped((rows, width), bf16),
        shaped((width, rows), bf16),
        shaped((rows, width), bf16),
        shaped((rows, 2 * KV), bf16),
        shaped((rows, 2 * LANES), f32),
        shaped((8, width), f32),
        shaped((width, QKV + 64), bf16),
    ]
    return call(
        project_kernel,
        "project",
        outs,
        [info, *got, *pieces],
        [SM] + [VM] * 8,
        [pltpu.VMEM((rows, got[0].shape[2]), bf16)],
        3e9,
    )


class Copies:
    def __init__(self, sems):
        self.sems, self.n, self.open = sems, 0, []

    def start(self, choices, target):
        self.begin([(condition, source, target) for condition, source in choices])

    def send(self, source, choices):
        self.begin([(condition, source, target) for condition, target in choices])

    def begin(self, choices):
        sem = self.sems.at[self.n]
        self.n += 1
        for condition, source, target in choices:
            copy = pltpu.make_async_copy(source, target, sem)
            if condition is None:
                copy.start()
            else:
                pl.when(condition)(copy.start)
        self.open.append(copy)

    def wait(self, count=None):
        count = len(self.open) if count is None else count
        for copy in self.open[:count]:
            copy.wait()
        self.open = self.open[count:]

    def keep_or_send(self, core, mine, source, keep, send):
        self.send(source, [(core == mine, keep), (core != mine, send)])


def start_out_weight(copies, f, pieces, target):
    rows, width = pieces[0].shape[0], target.shape[1]
    for piece, bit in zip(pieces, (0, 2, 1, 3)):
        there = pl.ds(pl.multiple_of((f ^ bit) * rows, 16), rows)
        copies.start([(None, piece.at[:, pl.ds(QKV + 64, width)])], target.at[there, :])


def branch_kernel(info, mixed, residual, gains, *refs):
    out_pieces, (hidden, normed, normed_t, w, sems) = refs[:4], refs[4:]
    copies = Copies(sems)
    start_out_weight(copies, info[0], out_pieces, w)
    copies.wait()
    width = hidden.shape[1]
    for c in range(0, width, 2 * LANES):
        here = slice(c, min(c + 2 * LANES, width))
        hidden[:, here] = residual[:, here] + dot(mixed[...], w[:, here])
    x = hidden[...]
    inverse = lax.rsqrt(jnp.mean(x * x, axis=-1, keepdims=True) + eps)
    n = x * inverse * gains[1:2, :]
    normed[...] = n.astype(bf16)
    normed_t[...] = n.T.astype(bf16)


def branch(info, mixed, residual, gains, out_pieces):
    rows, width = residual.shape
    return call(
        branch_kernel,
        "branch",
        [shaped((rows, width), f32), shaped((rows, width), bf16), shaped((width, rows), bf16)],
        [info, mixed, residual, gains, *out_pieces],
        [SM] + [VM] * 3 + [ANY] * 4,
        [pltpu.VMEM((width, width), bf16), pltpu.SemaphoreType.DMA((8,))],
        1.5e9,
    )


def ffn_kernel(h, first, info, normed, normed_t, grads, grads_by, result_in, back_in, *refs):
    gate_pieces, up_pieces, down_pieces, far_pieces, refs = (
        refs[:2], refs[2:4], refs[4:8], refs[8:10], refs[10:]
    )
    result, back, keep, send = refs[:4]
    wg, wu, wd, act_s, g_s, right_s, both_s, down_s, sems = refs[4:]
    f, x, core = info[0], info[0] // 2, info[0] % 2
    half = wg.shape[1]
    copies = Copies(sems)
    for k, (near, target) in enumerate(((gate_pieces, wg), (up_pieces, wu))):
        here, there = pl.ds(h * half, half), pl.ds(k * half, half)
        for bit, source in (
            (0, near[0].at[:, here]),
            (1, near[1].at[:, here]),
            (2, far_pieces[0].at[:, there]),
            (3, far_pieces[1].at[:, there]),
        ):
            rows = pl.ds(pl.multiple_of((f ^ bit) * 240, 16), 240)
            copies.start([(None, source)], target.at[rows, :])
    own, own_o, far, far_o = down_pieces
    n = half // 2
    for bit, near_ref, far_ref in ((0, own, far), (1, own_o, far_o)):
        there = pl.ds(pl.multiple_of((core ^ bit) * n, LANES), n)
        copies.start([(x == h, near_ref), (x != h, far_ref)], wd.at[:, there])
    copies.wait()
    step = 2 * LANES
    cols = half // 4
    for c in range(0, half, step):
        here = slice(c, c + step)
        gate = dot(normed[...], wg[:, here])
        up = dot(normed[...], wu[:, here])
        sigmoid = 1.0 / (1.0 + jnp.exp(-gate))
        act_s[:, here] = (gate * sigmoid * up).astype(bf16)
        grad_act = dot(grads[...], wd[:, here])
        g_s[:, c : c + step] = (
            grad_act * up * sigmoid * (1.0 + gate * (1.0 - sigmoid))
        ).astype(bf16)
        g_s[:, half + c : half + c + step] = (grad_act * gate * sigmoid).astype(bf16)
    for y in range(2):
        for z in range(2):
            for k in range(2):
                at = k * half + (2 * z + y) * cols
                to = ((2 * y + z) * 2 + k) * cols
                right_s[:, to : to + cols] = g_s[:, at : at + cols]
    for y in range(2):
        lanes = slice(y * half, (y + 1) * half)
        for c in range(y * half, (y + 1) * half, step):
            both_s[:, c : c + step] = dot(normed_t[...], right_s[:, c : c + step]).astype(bf16)
        for place in range(4):
            copies.keep_or_send(
                core,
                place % 2,
                both_s.at[pl.ds(place * 240, 240), pl.ds(y * half, half)],
                keep.at[pl.ds(place // 2 * 240, 240), pl.ds(y * half, half)],
                send.at[pl.ds(place // 2 * 240, 240), pl.ds(y * half, half)],
            )
    place = half // 2
    for c in range(0, half, step):
        down_s[:, c : c + step] = dot(grads_by[...], act_s[:, c : c + step]).astype(bf16)
    rows = down_s.shape[0] // 4
    for mine in range(2):
        for part in range(4):
            source = down_s.at[pl.ds(part * rows, rows), pl.ds(mine * place, place)]
            there = (pl.ds(480, rows), pl.ds(part * place, place))
            copies.keep_or_send(core, mine, source, keep.at[there], send.at[there])
    width = normed.shape[1]
    for c in range(0, width, step):
        here = slice(c, min(c + step, width))
        result[:, here] = result_in[:, here] + dot(act_s[...], wd[here, :], NT)
        out = dot(g_s[:, :half], wg[here, :], NT) + dot(g_s[:, half:], wu[here, :], NT)
        back[:, here] = out if first else back_in[:, here] + out
    copies.wait()


def ffn(h, info, normed, normed_t, grads, grads_by, result, back, gate_p, up_p, down_p, far_p):
    rows, width = result.shape
    half = 2 * down_p[0].shape[1]
    outs = [
        shaped((rows, width), f32 if h == 0 else bf16),
        shaped((rows, width), f32),
        shaped((480 + 2 * LANES, 2 * half), bf16),
        shaped((480 + 2 * LANES, 2 * half), bf16),
    ]

    def kernel(info, normed, normed_t, grads, grads_by, result_in, back_in, *refs):
        lists, result_ref, rest = refs[:10], refs[10], refs[11:]
        target = Rounded(result_ref) if h == 1 else result_ref
        ffn_kernel(
            h, h == 0, info, normed, normed_t, grads, grads_by, result_in, back_in,
            *lists, target, *rest,
        )

    return call(
        kernel,
        "ffn",
        outs,
        [info, normed, normed_t, grads, grads_by, result, back, *gate_p, *up_p, *down_p, *far_p],
        [SM] + [VM] * 6 + [ANY] * 10,
        [
            pltpu.VMEM((width, half), bf16),
            pltpu.VMEM((width, half), bf16),
            pltpu.VMEM((width, half), bf16),
            pltpu.VMEM((rows, half), bf16),
            pltpu.VMEM((rows, 2 * half), bf16),
            pltpu.VMEM((rows, 2 * half), bf16),
            pltpu.VMEM((width, 2 * half), bf16),
            pltpu.VMEM((8 * LANES, half), bf16),
            pltpu.SemaphoreType.DMA((28,)),
        ],
        11.5e9,
        far=(2, 3),
    )


class Rounded:
    def __init__(self, ref):
        self.ref = ref

    def __setitem__(self, index, value):
        self.ref[index] = value.astype(self.ref.dtype)


def fill_by_place(target, source, cols):
    target[...] = jnp.zeros_like(target)
    for y in range(2):
        for z in range(4):
            t, at = 2 * z + y, (4 * y + z) * LANES
            target[:, at : at + cols] = source[:, t * cols : (t + 1) * cols]


def order_kernel(info, *refs):
    got, (rows_ref, by_t_ref, by_ref) = refs[:4], refs[4:]
    sequence = info[1]
    block = got[0].shape[1]
    half = rows_ref.shape[0] // 2
    for r in range(4):
        i = lax.rem(sequence + 4 - r, 4)
        rows_ref[pl.ds(pl.multiple_of(i * block, block), block), :] = got[r][0]
        high = half + (3 - i) * block
        rows_ref[pl.ds(pl.multiple_of(high, block), block), :] = got[r][1]
    fill_by_place(by_ref, rows_ref, rows_ref.shape[1] // 8)
    by_t_ref[...] = by_ref[...].T


def order(info, got):
    rows, width = 8 * got[0].shape[1], got[0].shape[2]
    return call(
        order_kernel,
        "order",
        [shaped((rows, width), bf16), shaped((8 * LANES, rows), bf16)],
        [info, *got],
        [SM] + [VM] * 4,
        [pltpu.VMEM((rows, 8 * LANES), bf16)],
        1e7,
    )


def norm_back(x, gain, grad):
    inverse = lax.rsqrt(jnp.mean(x * x, axis=-1, keepdims=True) + eps)
    scaled = grad * gain
    gain_grad = jnp.sum(grad * x * inverse, axis=0, keepdims=True)
    out = inverse * scaled - x * inverse**3 * jnp.mean(scaled * x, axis=-1, keepdims=True)
    return out, gain_grad


def branch_back_kernel(info, hidden, back, grads, mixed_t, gains, *refs):
    out_pieces, refs = refs[:4], refs[4:]
    grad_hidden, grad_mixed, keep, send, gain_grad, w, low, by, out_s, sems = refs
    copies = Copies(sems)
    start_out_weight(copies, info[0], out_pieces, w)
    core = info[0] % 2
    width = hidden.shape[1]
    through, total = norm_back(hidden[...], gains[1:2, :], back[...])
    gain_grad[...] = jnp.broadcast_to(total, gain_grad.shape)
    out = grads[...].astype(f32) + through
    grad_hidden[...] = out
    low[...] = out.astype(bf16)
    fill_by_place(by, low, width // 8)
    copies.wait()
    step = 2 * LANES
    for c in range(0, width, step):
        here = slice(c, min(c + step, width))
        grad_mixed[:, here] = dot(low[...], w[here, :], NT).astype(bf16)
    for c in range(0, 8 * LANES, step):
        out_s[:, c : c + step] = dot(mixed_t[...], by[:, c : c + step]).astype(bf16)
    for place in range(4):
        source = out_s.at[pl.ds(place * 240, 240), :]
        there = place // 2
        copies.keep_or_send(core, place % 2, source, keep.at[there], send.at[there])
    copies.wait()


def branch_back(info, hidden, back, grads, mixed_t, gains, out_pieces):
    rows, width = hidden.shape
    return call(
        branch_back_kernel,
        "branch_back",
        [
            shaped((rows, width), f32),
            shaped((rows, width), bf16),
            shaped((2, 240, 8 * LANES), bf16),
            shaped((2, 240, 8 * LANES), bf16),
            shaped((8, width), f32),
        ],
        [info, hidden, back, grads, mixed_t, gains, *out_pieces],
        [SM] + [VM] * 5 + [ANY] * 4,
        [
            pltpu.VMEM((width, width), bf16),
            pltpu.VMEM((rows, width), bf16),
            pltpu.VMEM((rows, 8 * LANES), bf16),
            pltpu.VMEM((width, 8 * LANES), bf16),
            pltpu.SemaphoreType.DMA((12,)),
        ],
        3e9,
        far=(2, 3),
    )


def project_back_kernel(
    info, dq, own, other, tables, normed_t, residual, grad_hidden, gains, ffn_gain_grad, w, *refs
):
    input_grad, keep, send, g_s, by, back, spare, out_s, sems = refs
    core = info[0] % 2
    rows, width = dq.shape
    cosine, sine = tables[:, :LANES], tables[:, LANES:]
    sign = sine_signs(rows)
    low = lax.broadcasted_iota(jnp.int32, (rows, LANES), 1) < HEAD_SIZE

    def unturn(tile):
        return tile * cosine - turn(tile * sine, sign)

    for at in range(0, 2 * KV, LANES):
        tile = own[:, at : at + LANES] + other[:, at : at + LANES].astype(f32)
        if at + LANES <= KV:
            tile = unturn(tile)
        elif at < KV:
            tile = jnp.where(low, unturn(tile), tile)
        g_s[:, at : at + LANES] = tile.astype(bf16)
    for at in range(0, width, LANES):
        n = min(LANES, width - at)
        if n == LANES:
            tile = unturn(dq[:, at : at + LANES])
        else:
            half = dq[:, at : at + n]
            tile = unturn(jnp.concatenate([half, half], axis=1))[:, :n]
        g_s[:, 2 * KV + at : 2 * KV + at + n] = tile.astype(bf16)
    step = 2 * LANES
    for c in range(0, width, step):
        here = slice(c, min(c + step, width))
        back[:, here] = dot(g_s[...], w[here, :QKV], NT)
    through, gain_grad = norm_back(residual[...], gains[0:1, :], back[...])
    input_grad[...] = (grad_hidden[...] + through).astype(bf16)
    spare[...] = jnp.concatenate(
        [
            jnp.broadcast_to(gain_grad, (LANES // 2, width)),
            jnp.broadcast_to(ffn_gain_grad[0:1, :], (LANES // 2, width)),
        ],
        axis=0,
    ).T
    cols, kv_cols = width // 8, KV // 8
    first = cols + 2 * kv_cols
    by[...] = jnp.zeros_like(by)
    for y in range(2):
        for z in range(4):
            t, at = 2 * z + y, (4 * y + z) * step
            by[:, at : at + cols] = g_s[:, 2 * KV + t * cols : 2 * KV + (t + 1) * cols]
            at = at + cols
            by[:, at : at + kv_cols] = g_s[:, t * kv_cols : (t + 1) * kv_cols]
            at = at + kv_cols
            by[:, at : at + kv_cols] = g_s[:, KV + t * kv_cols : KV + (t + 1) * kv_cols]
    lane = lax.broadcasted_iota(jnp.int32, (width, step), 1)
    one, two = spare[:, 0:1], spare[:, LANES - 1 : LANES]
    for c in range(0, 8 * step, step):
        value = dot(normed_t[...], by[:, c : c + step])
        value = jnp.where(lane == first, one, value)
        out_s[:, c : c + step] = jnp.where(lane == first + 1, two, value).astype(bf16)
    copies = Copies(sems)
    for place in range(4):
        source = out_s.at[pl.ds(place * 240, 240), :]
        there = place // 2
        copies.keep_or_send(core, place % 2, source, keep.at[there], send.at[there])
    copies.wait()


def project_back(info, dq, own, other, tables, normed_t, residual, grad_hidden, gains, gain_grad, w):
    rows, width = dq.shape
    step = 2 * LANES
    return call(
        project_back_kernel,
        "project_back",
        [
            shaped((rows, width), bf16),
            shaped((2, 240, 8 * step), bf16),
            shaped((2, 240, 8 * step), bf16),
        ],
        [info, dq, own, other, tables, normed_t, residual, grad_hidden, gains, gain_grad, w],
        [SM] + [VM] * 10,
        [
            pltpu.VMEM((rows, QKV), bf16),
            pltpu.VMEM((rows, 8 * step), bf16),
            pltpu.VMEM((rows, width), f32),
            pltpu.VMEM((width, LANES), f32),
            pltpu.VMEM((width, 8 * step), bf16),
            pltpu.SemaphoreType.DMA((4,)),
        ],
        5e9,
        far=(1, 2),
    )


def shards_small(
    inputs,
    attn_gain,
    query_weight,
    key_projection_weight,
    value_projection_weight,
    out_weight,
    ffn_gain,
    gate_weight,
    up_weight,
    down_weight,
    positions,
    cotangent,
):
    seqs, _, _, block, width = inputs.shape
    lay = Layout(seqs)
    ff = gate_weight.shape[1]
    even = lay.t % 2 == 0
    member = lay.member.astype(jnp.int32).reshape(1)
    info = jnp.stack([lay.f, lay.sequence, lay.t % 2]).astype(jnp.int32)

    place = positions.reshape(seqs, 2, block, 1)
    tokens = inputs.reshape(seqs, 2, block, width)
    packed = jnp.concatenate(
        [tokens, (place // 128).astype(bf16), (place % 128).astype(bf16)], axis=-1
    )
    qkvg = jnp.concatenate(
        [
            key_projection_weight,
            value_projection_weight,
            query_weight,
            attn_gain[:, None],
            ffn_gain[:, None],
            jnp.zeros((attn_gain.shape[0], 62), bf16),
            out_weight,
        ],
        axis=1,
    )
    got = lay.receive(packed)
    far = swap(qkvg, "fsdp", 2)
    far, *got = lax.optimization_barrier((far, *got))
    qkvg_pieces = [qkvg, far, swap(qkvg, "fsdp", 1), swap(far, "fsdp", 1)]


    def ffn_part(h, *before):
        lanes = slice(h * ff // 2, (h + 1) * ff // 2)
        parts = gate_weight[:, lanes], up_weight[:, lanes]
        return after(jnp.concatenate(parts, axis=1), *before)

    far0 = swap(ffn_part(0, far), "fsdp", 2)

    residual, normed, normed_t, query, kv, tables, gains, w = project(info, got, qkvg_pieces, width)
    pieces = lay.gather_group(kv)
    far0, *pieces = lax.optimization_barrier((far0, *pieces))
    far0_o = swap(far0, "fsdp", 1)
    down_weight = after(down_weight.T, far0)
    down_far = swap(down_weight, "fsdp", 2)
    grad_got = lay.receive(after(cotangent.reshape(seqs, 2, block, width), residual))
    mixed, mixed_t, lse = attention_forward(member, query, pieces)
    mixed, *grad_got = lax.optimization_barrier((mixed, *grad_got))
    gate_weight, up_weight, down_weight = lax.optimization_barrier(
        (gate_weight, up_weight, down_weight, mixed)
    )[:3]
    far1 = swap(ffn_part(1, mixed), "fsdp", 2)
    gate_p = [gate_weight, swap(gate_weight, "fsdp", 1)]
    up_p = [up_weight, swap(up_weight, "fsdp", 1)]
    down_o = swap(down_weight, "fsdp", 1)
    hidden, normed_ffn, normed_ffn_t = branch(info, mixed, residual, gains, qkvg_pieces)
    grads, grads_by = order(info, grad_got)
    down_far, normed_ffn = lax.optimization_barrier((down_far, normed_ffn))
    down_far_o = swap(down_far, "fsdp", 1)
    down_p = [down_weight, down_o, down_far, down_far_o]

    sums = Sums()

    def over_core(keep, send):
        return add(keep, swap(send, "fsdp", 1))

    common = (info, normed_ffn, normed_ffn_t, grads, grads_by)
    result, back, keep0, send0 = ffn(
        0, *common, hidden, hidden, gate_p, up_p, down_p, [far0, far0_o]
    )
    far1, result = lax.optimization_barrier((far1, result))
    far1_o = swap(far1, "fsdp", 1)
    result, back, keep1, send1 = ffn(
        1, *common, result, back, gate_p, up_p, down_p, [far1, far1_o]
    )
    n = 2 * attn_gain.shape[0]
    core0 = over_core(keep0, send0)
    back, core0 = lax.optimization_barrier((back, core0))
    both0 = sums.over_x(core0[:n].reshape(2, n // 2, ff))
    grad_hidden, grad_mixed, out_k, out_s, ffn_gain_grad = branch_back(
        info, hidden, back, grads, mixed_t, gains, qkvg_pieces
    )
    core1 = over_core(keep1, send1)
    result = after(result, back)
    home = [lay.send_back(result, 0)]
    grad_mixed, core1 = lax.optimization_barrier((grad_mixed, core1))
    both1 = sums.over_y(core1[:n].reshape(2, n // 2, ff))
    down_sum = sums.halves(core0[n:], core1[n:], sums.x, "fsdp", 2)
    dq, dkv, dkv_send = attention_backward(member, query, pieces, mixed, grad_mixed, lse)
    dkv_other = lay.around(dkv_send, 1)
    dq, both0, both1, down_sum, result, *home = lax.optimization_barrier(
        (dq, both0, both1, down_sum, result, *home)
    )
    both0 = sums.over_y(both0)
    both1 = sums.over_x(both1)
    home += [lay.send_back(result, r) for r in range(1, seqs)]
    input_grad, qkv_k, qkv_s = project_back(
        info, dq, dkv, dkv_other, tables, normed_t, residual, grad_hidden, gains, ffn_gain_grad, w
    )
    qkv_s, out_s, *home = lax.optimization_barrier((qkv_s, out_s, *home))
    outputs = lay.place_back(home)
    qkv_sum = over_core(qkv_k, qkv_s)
    out_sum = over_core(out_k, out_s)
    qkv_sum, out_sum, both0, both1, down_sum = lax.optimization_barrier(
        (qkv_sum, out_sum, both0, both1, down_sum)
    )
    qkv_sum = sums.over_x(qkv_sum)
    out_sum = sums.over_y(out_sum)
    qkv_sum, out_sum, down_sum, input_grad = lax.optimization_barrier(
        (qkv_sum, out_sum, down_sum, input_grad)
    )
    down_sum = sums.over_y(down_sum)
    out_sum = sums.over_x(out_sum)
    input_grad = lay.from_sequence(input_grad)
    cols, kv_cols, ff_cols = width // 8, KV // 8, ff // 8
    half = 2 * ff_cols
    gate_up = sums.over_z(
        jnp.stack([b[:, i * half : (i + 1) * half] for b in (both0, both1) for i in range(2)])
    )
    qkv_sum = sums.over_y(qkv_sum)
    pieces = []
    for z in range(4):
        low = out_sum[:, z * LANES : (z + 1) * LANES]
        low = jnp.concatenate([low[i * 48 : (i + 1) * 48] for i in range(5)], axis=1)
        part = down_sum[z % 2 * LANES : (z % 2 + 1) * LANES, z // 2 * half : (z // 2 + 1) * half]
        wide = qkv_sum[:, 2 * z * LANES : 2 * (z + 1) * LANES]
        last = jnp.concatenate([wide[192:, :LANES], wide[192:, LANES:]])
        wide = jnp.concatenate([wide[:96], wide[96:192], last], axis=1)
        pieces.append(jnp.concatenate([part, low, wide]))
    rest = sums.over_z(jnp.stack(pieces))
    first = cols + 2 * kv_cols
    low, wide = rest[LANES : LANES + 48], rest[LANES + 48 :]
    out_grad = jnp.concatenate([low[:, i * LANES : i * LANES + cols] for i in range(5)])
    step = 2 * LANES
    last = jnp.concatenate([wide[:48, 2 * step :], wide[48:, 2 * step :]], axis=1)
    qkv_sum = jnp.concatenate([wide[:, :step], wide[:, step : 2 * step], last])
    return (
        outputs.reshape(inputs.shape),
        input_grad.astype(f32).reshape(inputs.shape),
        qkv_sum[:, first],
        qkv_sum[:, :cols],
        qkv_sum[:, cols : cols + kv_cols],
        qkv_sum[:, cols + kv_cols : first],
        out_grad,
        qkv_sum[:, first + 1],
        gate_up[:, :ff_cols],
        gate_up[:, ff_cols:],
        rest[:cols].T,
    )


def shards(
    inputs,
    attn_gain,
    query_weight,
    key_projection_weight,
    value_projection_weight,
    out_weight,
    ffn_gain,
    gate_weight,
    up_weight,
    down_weight,
    positions,
    cotangent,
):
    seqs, _, _, block, width = inputs.shape
    lay = Layout(seqs)
    place = positions.reshape(seqs, 2, block, 1)
    packed = jnp.concatenate(
        [
            inputs.reshape(seqs, 2, block, width),
            (place // 128).astype(bf16),
            (place % 128).astype(bf16),
        ],
        axis=-1,
    )
    packed = lay.to_sequence(packed)
    residual = packed[:, :width].astype(f32)
    place = packed[:, width].astype(f32) * 128.0 + packed[:, width + 1].astype(f32)
    member = lay.member.astype(jnp.int32).reshape(1)
    qkvg = jnp.concatenate(
        [
            query_weight,
            key_projection_weight,
            value_projection_weight,
            attn_gain[:, None],
            ffn_gain[:, None],
        ],
        axis=1,
    )
    qkvg_full, out_full, gate_full, up_full, down_full = [
        lax.all_gather(w, "fsdp", axis=0, tiled=True)
        for w in (qkvg, out_weight, gate_weight, up_weight, down_weight)
    ]
    qkv_full = qkvg_full[:, : width + 2 * KV]
    first_gain = qkvg_full[:, width + 2 * KV].astype(f32)
    second_gain = qkvg_full[:, width + 2 * KV + 1].astype(f32)

    cosine, sine = rope_tables(place)
    normalized, inverse_first = norm_forward(residual, first_gain)
    normed = normalized.astype(bf16)
    qkv = dot(normed, qkv_full)
    query = rotate_pairs(qkv[:, :width], cosine, sine).astype(bf16)
    keys = rotate_pairs(qkv[:, width : width + KV], cosine, sine).astype(bf16)
    values = qkv[:, width + KV :].astype(bf16)
    pieces = lay.gather_group(jnp.concatenate([keys, values], axis=1))
    grad_rows = lay.to_sequence(cotangent.reshape(seqs, 2, block, width))
    mixed, _, lse = attention_forward(member, query, pieces)
    hidden = residual + dot(mixed, out_full)
    normed_ffn, inverse_second = norm_forward(hidden, second_gain)
    normed_ffn = normed_ffn.astype(bf16)
    gate = dot(normed_ffn, gate_full)
    up = dot(normed_ffn, up_full)
    sigmoid = jax.nn.sigmoid(gate)
    act = (gate * sigmoid * up).astype(bf16)
    outputs = lay.from_sequence((hidden + dot(act, down_full)).astype(bf16))
    down_grad = dot(act, grad_rows, TN).astype(bf16)
    grad_act = dot(grad_rows, down_full, NT)
    grad_up = (grad_act * gate * sigmoid).astype(bf16)
    grad_gate = (grad_act * up * sigmoid * (1.0 + gate * (1.0 - sigmoid))).astype(bf16)
    gate_grad = dot(normed_ffn, grad_gate, TN).astype(bf16)
    up_grad = dot(normed_ffn, grad_up, TN).astype(bf16)
    grad_normed_ffn = dot(grad_gate, gate_full, NT) + dot(grad_up, up_full, NT)
    through, ffn_gain_grad = norm_backward(hidden, inverse_second, second_gain, grad_normed_ffn)
    grad_hidden = grad_rows.astype(f32) + through
    grad_branch = grad_hidden.astype(bf16)
    out_grad = dot(mixed, grad_branch, TN).astype(bf16)
    grad_mixed = dot(grad_branch, out_full, NT).astype(bf16)
    dq, dkv, *sends = attention_backward(member, query, pieces, mixed, grad_mixed, lse)
    dkv = lay.scatter_group(dkv, sends)
    grad_qkv = jnp.concatenate(
        [
            rotate_pairs_back(dq, cosine, sine).astype(bf16),
            rotate_pairs_back(dkv[:, :KV], cosine, sine).astype(bf16),
            dkv[:, KV:].astype(bf16),
        ],
        axis=1,
    )
    grad_normed = dot(grad_qkv, qkv_full, NT)
    grad_input, attn_gain_grad = norm_backward(residual, inverse_first, first_gain, grad_normed)
    input_grad = lay.from_sequence((grad_hidden + grad_input).astype(bf16))
    qkv_grad = dot(normed, grad_qkv, TN).astype(bf16)

    def scatter(grads):
        part = lax.psum_scatter(grads, "fsdp", scatter_dimension=0, tiled=True)
        return lax.psum_scatter(part, "ctx", scatter_dimension=1, tiled=True).astype(f32)

    down_grad, gate_grad, up_grad, out_grad, query_grad, key_grad, value_grad = [
        scatter(g)
        for g in (
            down_grad,
            gate_grad,
            up_grad,
            out_grad,
            qkv_grad[:, :width],
            qkv_grad[:, width : width + KV],
            qkv_grad[:, width + KV :],
        )
    ]
    gains = lax.psum(jnp.stack([attn_gain_grad, ffn_gain_grad]), ("ctx", "fsdp"))
    gain_rows = attn_gain.shape[0]
    gains = lax.dynamic_slice_in_dim(gains, lay.f * gain_rows, gain_rows, 1)
    return (
        outputs.reshape(inputs.shape),
        input_grad.astype(f32).reshape(inputs.shape),
        gains[0],
        query_grad,
        key_grad,
        value_grad,
        out_grad,
        gains[1],
        gate_grad,
        up_grad,
        down_grad,
    )


def solution(mesh):
    in_specs = (
        P("fsdp", "ctx", None, None, None),
        P("fsdp"),
        P("fsdp", None),
        P("fsdp", None),
        P("fsdp", None),
        P("fsdp", None),
        P("fsdp"),
        P("fsdp", None),
        P("fsdp", None),
        P("fsdp", None),
        P("fsdp", "ctx", None, None),
        P("fsdp", "ctx", None, None, None),
    )
    out_specs = (
        P("fsdp", "ctx", None, None, None),
        P("fsdp", "ctx", None, None, None),
        P("fsdp"),
        P("fsdp", "ctx"),
        P("fsdp", "ctx"),
        P("fsdp", "ctx"),
        P("fsdp", "ctx"),
        P("fsdp"),
        P("fsdp", "ctx"),
        P("fsdp", "ctx"),
        P("fsdp", "ctx"),
    )
    small = mesh.shape["fsdp"] == 4 and mesh.shape["ctx"] == 8
    return jax.shard_map(
        shards_small if small else shards, mesh=mesh, in_specs=in_specs, out_specs=out_specs, check_vma=False)
```

```python
import functools
import math

import jax
import jax.numpy as jnp
from jax import lax
from jax.experimental import pallas as pl
from jax.experimental.pallas import tpu as pltpu
from jax.sharding import PartitionSpec as P

QUERY_HEADS = 15
KEY_VALUE_HEADS = 5
HEAD_SIZE = 64
GROUP = QUERY_HEADS // KEY_VALUE_HEADS
KV = KEY_VALUE_HEADS * HEAD_SIZE
SCALE = HEAD_SIZE**-0.5
VMEM = 50 * 1024 * 1024

eps = 1e-05
theta_base = 100000.0
bf16, f32 = jnp.bfloat16, jnp.float32


def dot(left, right, contract=((1,), (0,))):
    return lax.dot_general(left, right, (contract, ((), ())), preferred_element_type=f32)


NT = ((1,), (1,))
TN = ((0,), (0,))


def query_quarter(half, member, quarters):
    return jnp.where(half == 0, member, quarters - 1 - member)


def split_heads(source, target, half_rows):
    for half in range(2):
        rows = slice(half * half_rows, (half + 1) * half_rows)
        for g in range(KEY_VALUE_HEADS):
            for i in range(GROUP):
                lane = (g * GROUP + i) * HEAD_SIZE
                yield half, g, slice(i * half_rows, (i + 1) * half_rows), rows, slice(
                    lane, lane + HEAD_SIZE
                )


def diagonal_mask(tq):
    key_at = lax.broadcasted_iota(jnp.int32, (tq, GROUP * tq), 0)
    query_at = lax.broadcasted_iota(jnp.int32, (tq, GROUP * tq), 1) % tq
    return key_at <= query_at


def place_pieces(member, pieces, target, tq):
    quarters = target.shape[0] // tq
    group = quarters // 2
    for r, piece in enumerate(pieces):
        m = lax.rem(member + group - r, group)
        target[pl.ds(pl.multiple_of(m * tq, tq), tq), :] = piece[0:tq, :]
        high = pl.multiple_of((quarters - 1 - m) * tq, tq)
        target[pl.ds(high, tq), :] = piece[tq : 2 * tq, :]


def forward_kernel(group, member_ref, q_ref, *refs):
    pieces, refs = refs[:group], refs[group:]
    mixed_ref, mixed_t_ref, lse_ref, kv_ref, qh, top_s, sum_s, acc_s = refs
    tq = q_ref.shape[0] // 2
    quarters = 2 * group
    member = member_ref[0]
    place_pieces(member, pieces, kv_ref, tq)
    for half, g, hr, rows, lanes in split_heads(q_ref, qh, tq):
        qh[half, g, hr, :] = q_ref[rows, lanes] * jnp.asarray(SCALE, bf16)

    def one_half(half, _):
        own = query_quarter(half, member, quarters)

        def tile(ki, first):
            rows = pl.ds(pl.multiple_of(ki * tq, tq), tq)
            for g in range(KEY_VALUE_HEADS):
                keys = kv_ref[rows, g * HEAD_SIZE : (g + 1) * HEAD_SIZE]
                values = kv_ref[rows, KV + g * HEAD_SIZE : KV + (g + 1) * HEAD_SIZE]
                scores = dot(keys, qh[half, g], NT)
                if first:
                    scores = jnp.where(diagonal_mask(tq), scores, -1e30)
                    top = jnp.max(scores, axis=0, keepdims=True)
                    weights = jnp.exp(scores - top)
                    sum_s[g] = jnp.sum(weights, axis=0, keepdims=True)
                    acc_s[g] = dot(values, weights.astype(bf16), TN)
                else:
                    before = top_s[g]
                    top = jnp.maximum(before, jnp.max(scores, axis=0, keepdims=True))
                    weights = jnp.exp(scores - top)
                    fade = jnp.exp(before - top)
                    sum_s[g] = sum_s[g] * fade + jnp.sum(weights, axis=0, keepdims=True)
                    acc_s[g] = acc_s[g] * fade + dot(values, weights.astype(bf16), TN)
                top_s[g] = top

        tile(own, True)

        def body(ki, _):
            tile(ki, False)
            return 0

        lax.fori_loop(0, own, body, 0)
        rows = pl.ds(pl.multiple_of(half * tq, tq), tq)
        for g in range(KEY_VALUE_HEADS):
            total = sum_s[g]
            mixed_t = acc_s[g] / total
            mixed = mixed_t.T
            lse_ref[half, g] = top_s[g] + jnp.log(total)
            for i in range(GROUP):
                lane = (g * GROUP + i) * HEAD_SIZE
                here = slice(i * tq, (i + 1) * tq)
                mixed_ref[rows, lane : lane + HEAD_SIZE] = mixed[here].astype(bf16)
                mixed_t_ref[lane : lane + HEAD_SIZE, rows] = mixed_t[:, here].astype(bf16)
        return 0

    lax.fori_loop(0, 2, one_half, 0)


VM = pl.BlockSpec(memory_space=pltpu.VMEM)
SM = pl.BlockSpec(memory_space=pltpu.SMEM)
ANY = pl.BlockSpec(memory_space=pl.ANY)


def call(kernel, name, outs, ins, specs, scratch, flops, special=0, far=()):
    moved = sum(i.size * i.dtype.itemsize for i in ins)
    moved += sum(o.size * o.dtype.itemsize for o in outs)
    return pl.pallas_call(
        kernel,
        out_shape=tuple(outs),
        in_specs=specs,
        out_specs=tuple(ANY if i in far else VM for i in range(len(outs))),
        scratch_shapes=scratch,
        compiler_params=pltpu.CompilerParams(vmem_limit_bytes=VMEM),
        cost_estimate=pl.CostEstimate(
            flops=int(flops), bytes_accessed=int(moved), transcendentals=int(special)
        ),
        name=name,
    )(*ins)


def shaped(dims, kind):
    return jax.ShapeDtypeStruct(dims, kind)


def attention_forward(member, query, pieces):
    rows, width = query.shape
    tq, group = rows // 2, len(pieces)
    row = (KEY_VALUE_HEADS, 1, GROUP * tq)
    return call(
        functools.partial(forward_kernel, group),
        "attention_forward",
        [shaped((rows, width), bf16), shaped((width, rows), bf16), shaped((2,) + row, f32)],
        [member, query, *pieces],
        [SM] + [VM] * (1 + group),
        [
            pltpu.VMEM((2 * group * tq, 2 * KV), bf16),
            pltpu.VMEM((2, KEY_VALUE_HEADS, GROUP * tq, HEAD_SIZE), bf16),
            pltpu.VMEM(row, f32),
            pltpu.VMEM(row, f32),
            pltpu.VMEM((KEY_VALUE_HEADS, HEAD_SIZE, GROUP * tq), f32),
        ],
        8e9,
        4e6,
    )


def backward_kernel(group, member_ref, q_ref, *refs):
    pieces, refs = refs[:group], refs[group:]
    (mixed_ref, grad_ref, lse_ref, dq_ref, own_ref), refs = refs[:5], refs[5:]
    send_refs, refs = refs[: group - 1], refs[group - 1 :]
    kv_ref, qh, gh, delta, dq_s, dk_s, dv_s = refs
    tq = q_ref.shape[0] // 2
    quarters = 2 * group
    member = member_ref[0]
    place_pieces(member, pieces, kv_ref, tq)
    ones = jnp.ones((8, HEAD_SIZE), bf16)
    for half, g, hr, rows, lanes in split_heads(q_ref, qh, tq):
        qh[half, g, hr, :] = q_ref[rows, lanes] * jnp.asarray(SCALE, bf16)
        grads = grad_ref[rows, lanes]
        gh[half, g, hr, :] = grads
        product = grads.astype(f32) * mixed_ref[rows, lanes].astype(f32)
        high = product.astype(bf16)
        low = (product - high.astype(f32)).astype(bf16)
        delta[half, g, :, hr] = (dot(ones, high, NT) + dot(ones, low, NT))[0:1]
    dk_s[...] = jnp.zeros_like(dk_s)
    dv_s[...] = jnp.zeros_like(dv_s)

    def one_half(half, _):
        own = query_quarter(half, member, quarters)

        def tile(ki, first):
            rows = pl.ds(pl.multiple_of(ki * tq, tq), tq)
            for g in range(KEY_VALUE_HEADS):
                keys = kv_ref[rows, g * HEAD_SIZE : (g + 1) * HEAD_SIZE]
                values = kv_ref[rows, KV + g * HEAD_SIZE : KV + (g + 1) * HEAD_SIZE]
                query = qh[half, g]
                grads = gh[half, g]
                probs = jnp.exp(dot(keys, query, NT) - lse_ref[half, g])
                if first:
                    probs = jnp.where(diagonal_mask(tq), probs, 0.0)
                grad_probs = dot(values, grads, NT)
                dv_s[g, rows, :] += dot(probs.astype(bf16), grads)
                grad_scores = (probs * (grad_probs - delta[half, g])).astype(bf16)
                dk_s[g, rows, :] += dot(grad_scores, query)
                dq = dot(keys, grad_scores, TN)
                if first:
                    dq_s[g] = dq
                else:
                    dq_s[g] += dq

        tile(own, True)

        def body(ki, _):
            tile(ki, False)
            return 0

        lax.fori_loop(0, own, body, 0)
        rows = pl.ds(pl.multiple_of(half * tq, tq), tq)
        for g in range(KEY_VALUE_HEADS):
            dq = (dq_s[g] * SCALE).T
            for i in range(GROUP):
                lane = (g * GROUP + i) * HEAD_SIZE
                dq_ref[rows, lane : lane + HEAD_SIZE] = dq[i * tq : (i + 1) * tq]
        return 0

    lax.fori_loop(0, 2, one_half, 0)
    for r, target in enumerate((own_ref,) + tuple(send_refs)):
        m = lax.rem(member + r, group)
        for part, quarter in ((0, m), (1, quarters - 1 - m)):
            rows = pl.ds(pl.multiple_of(quarter * tq, tq), tq)
            there = slice(part * tq, (part + 1) * tq)
            for g in range(KEY_VALUE_HEADS):
                lane = g * HEAD_SIZE
                target[there, lane : lane + HEAD_SIZE] = dk_s[g, rows, :].astype(target.dtype)
                lane = KV + g * HEAD_SIZE
                target[there, lane : lane + HEAD_SIZE] = dv_s[g, rows, :].astype(target.dtype)


def attention_backward(member, query, pieces, mixed, grad_mixed, lse):
    rows, width = query.shape
    tq, group = rows // 2, len(pieces)
    heads = (2, KEY_VALUE_HEADS, GROUP * tq, HEAD_SIZE)
    total = 2 * group * tq
    outs = [shaped((rows, width), f32), shaped((rows, 2 * KV), f32)]
    return call(
        functools.partial(backward_kernel, group),
        "attention_backward",
        outs + [shaped((rows, 2 * KV), bf16)] * (group - 1),
        [member, query, *pieces, mixed, grad_mixed, lse],
        [SM] + [VM] * (4 + group),
        [
            pltpu.VMEM((total, 2 * KV), bf16),
            pltpu.VMEM(heads, bf16),
            pltpu.VMEM(heads, bf16),
            pltpu.VMEM((2, KEY_VALUE_HEADS, 1, GROUP * tq), f32),
            pltpu.VMEM((KEY_VALUE_HEADS, HEAD_SIZE, GROUP * tq), f32),
            pltpu.VMEM((KEY_VALUE_HEADS, total, HEAD_SIZE), f32),
            pltpu.VMEM((KEY_VALUE_HEADS, total, HEAD_SIZE), f32),
        ],
        16e9,
        4e6,
    )


def rope_tables(positions):
    half = HEAD_SIZE // 2
    freqs = theta_base ** (-jnp.arange(half, dtype=f32) * 2.0 / HEAD_SIZE)
    angles = positions[:, None] * freqs
    cosine, sine = jnp.cos(angles), jnp.sin(angles)
    return jnp.concatenate([cosine, cosine], axis=1), jnp.concatenate([sine, sine], axis=1)


def rotate(rows):
    half = HEAD_SIZE // 2
    width = rows.shape[1]
    ahead = jnp.concatenate([rows[:, half:], rows[:, :half]], axis=1)
    behind = jnp.concatenate([rows[:, width - half :], rows[:, : width - half]], axis=1)
    lane = lax.broadcasted_iota(jnp.int32, rows.shape, 1) % HEAD_SIZE
    return jnp.where(lane < half, -ahead, behind)


def widen(table, width):
    return jnp.concatenate([table] * (width // HEAD_SIZE), axis=1)


def rotate_pairs(rows, cosine, sine):
    width = rows.shape[1]
    return rows * widen(cosine, width) + rotate(rows) * widen(sine, width)


def rotate_pairs_back(grads, cosine, sine):
    width = grads.shape[1]
    return grads * widen(cosine, width) - rotate(grads * widen(sine, width))


def norm_forward(rows, gain):
    inverse = lax.rsqrt(jnp.mean(rows * rows, axis=-1, keepdims=True) + eps)
    return rows * inverse * gain, inverse


def norm_backward(rows, inverse, gain, grad_normed):
    scaled = grad_normed * gain
    gain_grad = jnp.sum(grad_normed * rows * inverse, axis=0)
    value_grad = inverse * scaled - rows * inverse**3 * jnp.mean(
        scaled * rows, axis=-1, keepdims=True
    )
    return value_grad, gain_grad


class Layout:
    def __init__(self, seqs):
        self.S = seqs
        self.Pn = lax.axis_size("ctx")
        self.F = lax.axis_size("fsdp")
        self.places = self.Pn // (2 * seqs)
        self.G = 2 * self.places
        self.t = lax.axis_index("ctx")
        self.f = lax.axis_index("fsdp")
        core = self.f % 2
        self.member = (self.t % self.places) * 2 + core
        self.sequence = (self.t // self.places) % seqs

    def spread(self, r):
        pairs = []
        for u in range(self.Pn):
            for f in range(self.F):
                s = (u % self.S + r) % self.S
                m = u // self.S
                t = ((f % 2) * self.S + s) * self.places + m // 2
                pairs.append((u * self.F + f, t * self.F + (f // 2) * 2 + m % 2))
        return pairs

    def ring(self, r):
        pairs = []
        for t in range(self.Pn):
            for f in range(self.F):
                base = t - t % self.places
                m = ((t % self.places) * 2 + f % 2 + r) % self.G
                pairs.append((t * self.F + f, (base + m // 2) * self.F + (f // 2) * 2 + m % 2))
        return pairs

    def receive(self, array):
        got = []
        for r in range(self.S):
            piece = lax.dynamic_index_in_dim(
                array, (self.t % self.S + r) % self.S, 0, keepdims=False
            )
            got.append(lax.ppermute(piece, ("ctx", "fsdp"), self.spread(r)))
        return got

    def to_sequence(self, array):
        got = self.receive(array)
        ordered = jnp.stack(got[::-1] + got[::-1])
        start = (self.S - 1 - self.sequence) % self.S
        ordered = lax.dynamic_slice_in_dim(ordered, start, self.S, 0)
        low, high = ordered[:, 0], ordered[::-1, 1]
        block, width = array.shape[2], array.shape[3]
        return jnp.concatenate(
            [low.reshape(self.S * block, width), high.reshape(self.S * block, width)], axis=0
        )

    def from_sequence(self, rows):
        return self.place_back([self.send_back(rows, r) for r in range(self.S)])

    def send_back(self, rows, r):
        width = rows.shape[1]
        block = rows.shape[0] // (2 * self.S)
        halves = rows.reshape(2, self.S, block, width)
        slot = (self.sequence - r + self.S) % self.S
        low = lax.dynamic_index_in_dim(halves[0], slot, 0, keepdims=False)
        high = lax.dynamic_index_in_dim(halves[1], self.S - 1 - slot, 0, keepdims=False)
        back = [(b, a) for a, b in self.spread(r)]
        return lax.ppermute(jnp.stack([low, high]), ("ctx", "fsdp"), back)

    def place_back(self, got):
        ordered = jnp.stack(got + got)
        start = (self.S - self.t % self.S) % self.S
        return lax.dynamic_slice_in_dim(ordered, start, self.S, 0)

    def around(self, rows, r):
        return lax.ppermute(rows, ("ctx", "fsdp"), self.ring(r))

    def gather_group(self, rows):
        return [rows] + [self.around(rows, r) for r in range(1, self.G)]

    def scatter_group(self, own, sends):
        for r, piece in enumerate(sends):
            own = own + self.around(piece, r + 1).astype(f32)
        return own


def swap(array, axis, bit):
    size = lax.axis_size(axis)
    return lax.ppermute(array, axis, [(i, i ^ bit) for i in range(size)])


def after(array, *others):
    return lax.optimization_barrier((array,) + others)[0]


def add(one, other):
    return (one.astype(f32) + other.astype(f32)).astype(bf16)


class Sums:
    def __init__(self):
        f, t = lax.axis_index("fsdp"), lax.axis_index("ctx")
        self.core, self.x, self.y, self.z = f % 2, f // 2, t % 2, t // 2

    def exchange(self, mine, theirs, axis, bit):
        return add(mine, swap(theirs, axis, bit))

    def over_x(self, parts):
        return self.halves(parts[0], parts[1], self.x, "fsdp", 2)

    def halves(self, low, high, bit, axis, shift):
        flag = bit == 0
        return self.exchange(
            jnp.where(flag, low, high), jnp.where(flag, high, low), axis, shift
        )

    def lanes(self, parts, bit, axis, shift):
        half = parts.shape[-1] // 2
        return self.halves(parts[..., :half], parts[..., half:], bit, axis, shift)

    def over_y(self, parts):
        return self.lanes(parts, self.y, "ctx", 1)

    def over_z(self, parts, first=0):
        n = parts.shape[0]

        def part(z):
            return lax.dynamic_index_in_dim(parts, jnp.clip(z - first, 0, n - 1), 0, keepdims=False)

        total = part(self.z).astype(f32)
        for k in range(1, 4):
            pairs = [(t, (t + 2 * k) % 8) for t in range(8)]
            pairs = [(a, b) for a, b in pairs if first <= b // 2 < first + n]
            total = total + lax.ppermute(part((self.z + k) % 4), "ctx", pairs).astype(f32)
        return total


LANES = 128
QKV = 2 * KV + QUERY_HEADS * HEAD_SIZE


def turn(rows, sine_sign):
    half = HEAD_SIZE // 2
    ahead = pltpu.roll(rows, LANES - half, 1)
    behind = pltpu.roll(rows, half, 1)
    return jnp.where(sine_sign < 0, -ahead, behind)


def sine_signs(rows):
    lane = lax.broadcasted_iota(jnp.int32, (rows, LANES), 1) % HEAD_SIZE
    return jnp.where(lane < HEAD_SIZE // 2, -1.0, 1.0)


def project_kernel(info, *refs):
    got, refs = refs[:4], refs[4:]
    pieces, refs = refs[:4], refs[4:]
    residual, normed, normed_t, query, kv, tables, gains, w, tok = refs
    f, sequence = info[0], info[1]
    slots, block = 4, got[0].shape[1]
    rows, width = residual.shape
    half = rows // 2
    for r in range(slots):
        i = lax.rem(sequence + slots - r, slots)
        tok[pl.ds(pl.multiple_of(i * block, block), block), :] = got[r][0]
        high = half + (slots - 1 - i) * block
        tok[pl.ds(pl.multiple_of(high, block), block), :] = got[r][1]
    part = pieces[0].shape[0]
    for piece, bit in zip(pieces, (0, 2, 1, 3)):
        w[pl.ds(pl.multiple_of((f ^ bit) * part, 16), part), :] = piece[:, : QKV + 64]
    gains_t = w[:, QKV - 64 : QKV + 64].astype(f32).T
    gains[...] = jnp.broadcast_to(gains_t[64:65], gains.shape)
    gains[1:2, :] = gains_t[65:66]
    x = tok[:, :width].astype(f32)
    residual[...] = x
    place = tok[:, width : width + 1].astype(f32) * 128.0 + tok[:, width + 1 : width + 2].astype(f32)
    lane = lax.broadcasted_iota(jnp.int32, (1, LANES), 1) % (HEAD_SIZE // 2)
    freqs = jnp.exp(lane.astype(f32) * (-2.0 / HEAD_SIZE * math.log(theta_base)))
    angles = place * freqs
    cosine, sine = jnp.cos(angles), jnp.sin(angles)
    tables[:, :LANES] = cosine
    tables[:, LANES:] = sine
    inverse = lax.rsqrt(jnp.mean(x * x, axis=-1, keepdims=True) + eps)
    n = x * inverse * gains[0:1, :]
    normed[...] = n.astype(bf16)
    normed_t[...] = n.T.astype(bf16)
    sign = sine_signs(rows)
    low = lax.broadcasted_iota(jnp.int32, (rows, LANES), 1) < HEAD_SIZE
    for c in range(0, QKV, 2 * LANES):
        out = dot(normed[...], w[:, c : min(c + 2 * LANES, QKV + 64)])
        for at in (c, c + LANES):
            if at >= QKV:
                continue
            tile = out[:, at - c : at - c + LANES]
            turned = tile * cosine + turn(tile, sign) * sine
            if at + LANES <= KV:
                kv[:, at : at + LANES] = turned.astype(bf16)
            elif at < KV:
                kv[:, at : at + LANES] = jnp.where(low, turned, tile).astype(bf16)
            elif at < 2 * KV:
                kv[:, at : at + LANES] = tile.astype(bf16)
            else:
                q = at - 2 * KV
                n_lanes = min(LANES, width - q)
                query[:, q : q + n_lanes] = turned[:, :n_lanes].astype(bf16)


def project(info, got, pieces, width):
    rows = 8 * got[0].shape[1]
    outs = [
        shaped((rows, width), f32),
        shaped((rows, width), bf16),
        shaped((width, rows), bf16),
        shaped((rows, width), bf16),
        shaped((rows, 2 * KV), bf16),
        shaped((rows, 2 * LANES), f32),
        shaped((8, width), f32),
        shaped((width, QKV + 64), bf16),
    ]
    return call(
        project_kernel,
        "project",
        outs,
        [info, *got, *pieces],
        [SM] + [VM] * 8,
        [pltpu.VMEM((rows, got[0].shape[2]), bf16)],
        3e9,
    )


class Copies:
    def __init__(self, sems):
        self.sems, self.n, self.open = sems, 0, []

    def start(self, choices, target):
        self.begin([(condition, source, target) for condition, source in choices])

    def send(self, source, choices):
        self.begin([(condition, source, target) for condition, target in choices])

    def begin(self, choices):
        sem = self.sems.at[self.n]
        self.n += 1
        for condition, source, target in choices:
            copy = pltpu.make_async_copy(source, target, sem)
            if condition is None:
                copy.start()
            else:
                pl.when(condition)(copy.start)
        self.open.append(copy)

    def wait(self, count=None):
        count = len(self.open) if count is None else count
        for copy in self.open[:count]:
            copy.wait()
        self.open = self.open[count:]

    def keep_or_send(self, core, mine, source, keep, send):
        self.send(source, [(core == mine, keep), (core != mine, send)])


def start_out_weight(copies, f, pieces, target):
    rows, width = pieces[0].shape[0], target.shape[1]
    for piece, bit in zip(pieces, (0, 2, 1, 3)):
        there = pl.ds(pl.multiple_of((f ^ bit) * rows, 16), rows)
        copies.start([(None, piece.at[:, pl.ds(QKV + 64, width)])], target.at[there, :])


def branch_kernel(info, mixed, residual, gains, *refs):
    out_pieces, (hidden, normed, normed_t, w, sems) = refs[:4], refs[4:]
    copies = Copies(sems)
    start_out_weight(copies, info[0], out_pieces, w)
    copies.wait()
    width = hidden.shape[1]
    for c in range(0, width, 2 * LANES):
        here = slice(c, min(c + 2 * LANES, width))
        hidden[:, here] = residual[:, here] + dot(mixed[...], w[:, here])
    x = hidden[...]
    inverse = lax.rsqrt(jnp.mean(x * x, axis=-1, keepdims=True) + eps)
    n = x * inverse * gains[1:2, :]
    normed[...] = n.astype(bf16)
    normed_t[...] = n.T.astype(bf16)


def branch(info, mixed, residual, gains, out_pieces):
    rows, width = residual.shape
    return call(
        branch_kernel,
        "branch",
        [shaped((rows, width), f32), shaped((rows, width), bf16), shaped((width, rows), bf16)],
        [info, mixed, residual, gains, *out_pieces],
        [SM] + [VM] * 3 + [ANY] * 4,
        [pltpu.VMEM((width, width), bf16), pltpu.SemaphoreType.DMA((8,))],
        1.5e9,
    )


def ffn_kernel(h, first, info, normed, normed_t, grads, grads_by, result_in, back_in, *refs):
    gate_pieces, up_pieces, down_pieces, far_pieces, refs = (
        refs[:2], refs[2:4], refs[4:8], refs[8:10], refs[10:]
    )
    result, back, keep, send = refs[:4]
    wg, wu, wd, act_s, g_s, right_s, both_s, down_s, sems = refs[4:]
    f, x, core = info[0], info[0] // 2, info[0] % 2
    half = wg.shape[1]
    copies = Copies(sems)
    for k, (near, target) in enumerate(((gate_pieces, wg), (up_pieces, wu))):
        here, there = pl.ds(h * half, half), pl.ds(k * half, half)
        for bit, source in (
            (0, near[0].at[:, here]),
            (1, near[1].at[:, here]),
            (2, far_pieces[0].at[:, there]),
            (3, far_pieces[1].at[:, there]),
        ):
            rows = pl.ds(pl.multiple_of((f ^ bit) * 240, 16), 240)
            copies.start([(None, source)], target.at[rows, :])
    own, own_o, far, far_o = down_pieces
    n = half // 2
    for bit, near_ref, far_ref in ((0, own, far), (1, own_o, far_o)):
        there = pl.ds(pl.multiple_of((core ^ bit) * n, LANES), n)
        copies.start([(x == h, near_ref), (x != h, far_ref)], wd.at[:, there])
    copies.wait()
    step = 2 * LANES
    cols = half // 4
    for c in range(0, half, step):
        here = slice(c, c + step)
        gate = dot(normed[...], wg[:, here])
        up = dot(normed[...], wu[:, here])
        sigmoid = 1.0 / (1.0 + jnp.exp(-gate))
        act_s[:, here] = (gate * sigmoid * up).astype(bf16)
        grad_act = dot(grads[...], wd[:, here])
        g_s[:, c : c + step] = (
            grad_act * up * sigmoid * (1.0 + gate * (1.0 - sigmoid))
        ).astype(bf16)
        g_s[:, half + c : half + c + step] = (grad_act * gate * sigmoid).astype(bf16)
    for y in range(2):
        for z in range(2):
            for k in range(2):
                at = k * half + (2 * z + y) * cols
                to = ((2 * y + z) * 2 + k) * cols
                right_s[:, to : to + cols] = g_s[:, at : at + cols]
    for y in range(2):
        lanes = slice(y * half, (y + 1) * half)
        for c in range(y * half, (y + 1) * half, step):
            both_s[:, c : c + step] = dot(normed_t[...], right_s[:, c : c + step]).astype(bf16)
        for place in range(4):
            copies.keep_or_send(
                core,
                place % 2,
                both_s.at[pl.ds(place * 240, 240), pl.ds(y * half, half)],
                keep.at[pl.ds(place // 2 * 240, 240), pl.ds(y * half, half)],
                send.at[pl.ds(place // 2 * 240, 240), pl.ds(y * half, half)],
            )
    place = half // 2
    for c in range(0, half, step):
        down_s[:, c : c + step] = dot(grads_by[...], act_s[:, c : c + step]).astype(bf16)
    rows = down_s.shape[0] // 4
    for mine in range(2):
        for part in range(4):
            source = down_s.at[pl.ds(part * rows, rows), pl.ds(mine * place, place)]
            there = (pl.ds(480, rows), pl.ds(part * place, place))
            copies.keep_or_send(core, mine, source, keep.at[there], send.at[there])
    width = normed.shape[1]
    for c in range(0, width, step):
        here = slice(c, min(c + step, width))
        result[:, here] = result_in[:, here] + dot(act_s[...], wd[here, :], NT)
        out = dot(g_s[:, :half], wg[here, :], NT) + dot(g_s[:, half:], wu[here, :], NT)
        back[:, here] = out if first else back_in[:, here] + out
    copies.wait()


def ffn(h, info, normed, normed_t, grads, grads_by, result, back, gate_p, up_p, down_p, far_p):
    rows, width = result.shape
    half = 2 * down_p[0].shape[1]
    outs = [
        shaped((rows, width), f32 if h == 0 else bf16),
        shaped((rows, width), f32),
        shaped((480 + 2 * LANES, 2 * half), bf16),
        shaped((480 + 2 * LANES, 2 * half), bf16),
    ]

    def kernel(info, normed, normed_t, grads, grads_by, result_in, back_in, *refs):
        lists, result_ref, rest = refs[:10], refs[10], refs[11:]
        target = Rounded(result_ref) if h == 1 else result_ref
        ffn_kernel(
            h, h == 0, info, normed, normed_t, grads, grads_by, result_in, back_in,
            *lists, target, *rest,
        )

    return call(
        kernel,
        "ffn",
        outs,
        [info, normed, normed_t, grads, grads_by, result, back, *gate_p, *up_p, *down_p, *far_p],
        [SM] + [VM] * 6 + [ANY] * 10,
        [
            pltpu.VMEM((width, half), bf16),
            pltpu.VMEM((width, half), bf16),
            pltpu.VMEM((width, half), bf16),
            pltpu.VMEM((rows, half), bf16),
            pltpu.VMEM((rows, 2 * half), bf16),
            pltpu.VMEM((rows, 2 * half), bf16),
            pltpu.VMEM((width, 2 * half), bf16),
            pltpu.VMEM((8 * LANES, half), bf16),
            pltpu.SemaphoreType.DMA((28,)),
        ],
        11.5e9,
        far=(2, 3),
    )


class Rounded:
    def __init__(self, ref):
        self.ref = ref

    def __setitem__(self, index, value):
        self.ref[index] = value.astype(self.ref.dtype)


def fill_by_place(target, source, cols):
    target[...] = jnp.zeros_like(target)
    for y in range(2):
        for z in range(4):
            t, at = 2 * z + y, (4 * y + z) * LANES
            target[:, at : at + cols] = source[:, t * cols : (t + 1) * cols]


def order_kernel(info, *refs):
    got, (rows_ref, by_t_ref, by_ref) = refs[:4], refs[4:]
    sequence = info[1]
    block = got[0].shape[1]
    half = rows_ref.shape[0] // 2
    for r in range(4):
        i = lax.rem(sequence + 4 - r, 4)
        rows_ref[pl.ds(pl.multiple_of(i * block, block), block), :] = got[r][0]
        high = half + (3 - i) * block
        rows_ref[pl.ds(pl.multiple_of(high, block), block), :] = got[r][1]
    fill_by_place(by_ref, rows_ref, rows_ref.shape[1] // 8)
    by_t_ref[...] = by_ref[...].T


def order(info, got):
    rows, width = 8 * got[0].shape[1], got[0].shape[2]
    return call(
        order_kernel,
        "order",
        [shaped((rows, width), bf16), shaped((8 * LANES, rows), bf16)],
        [info, *got],
        [SM] + [VM] * 4,
        [pltpu.VMEM((rows, 8 * LANES), bf16)],
        1e7,
    )


def norm_back(x, gain, grad):
    inverse = lax.rsqrt(jnp.mean(x * x, axis=-1, keepdims=True) + eps)
    scaled = grad * gain
    gain_grad = jnp.sum(grad * x * inverse, axis=0, keepdims=True)
    out = inverse * scaled - x * inverse**3 * jnp.mean(scaled * x, axis=-1, keepdims=True)
    return out, gain_grad


def branch_back_kernel(info, hidden, back, grads, mixed_t, gains, *refs):
    out_pieces, refs = refs[:4], refs[4:]
    grad_hidden, grad_mixed, keep, send, gain_grad, w, low, by, out_s, sems = refs
    copies = Copies(sems)
    start_out_weight(copies, info[0], out_pieces, w)
    core = info[0] % 2
    width = hidden.shape[1]
    through, total = norm_back(hidden[...], gains[1:2, :], back[...])
    gain_grad[...] = jnp.broadcast_to(total, gain_grad.shape)
    out = grads[...].astype(f32) + through
    grad_hidden[...] = out
    low[...] = out.astype(bf16)
    fill_by_place(by, low, width // 8)
    copies.wait()
    step = 2 * LANES
    for c in range(0, width, step):
        here = slice(c, min(c + step, width))
        grad_mixed[:, here] = dot(low[...], w[here, :], NT).astype(bf16)
    for c in range(0, 8 * LANES, step):
        out_s[:, c : c + step] = dot(mixed_t[...], by[:, c : c + step]).astype(bf16)
    for place in range(4):
        source = out_s.at[pl.ds(place * 240, 240), :]
        there = place // 2
        copies.keep_or_send(core, place % 2, source, keep.at[there], send.at[there])
    copies.wait()


def branch_back(info, hidden, back, grads, mixed_t, gains, out_pieces):
    rows, width = hidden.shape
    return call(
        branch_back_kernel,
        "branch_back",
        [
            shaped((rows, width), f32),
            shaped((rows, width), bf16),
            shaped((2, 240, 8 * LANES), bf16),
            shaped((2, 240, 8 * LANES), bf16),
            shaped((8, width), f32),
        ],
        [info, hidden, back, grads, mixed_t, gains, *out_pieces],
        [SM] + [VM] * 5 + [ANY] * 4,
        [
            pltpu.VMEM((width, width), bf16),
            pltpu.VMEM((rows, width), bf16),
            pltpu.VMEM((rows, 8 * LANES), bf16),
            pltpu.VMEM((width, 8 * LANES), bf16),
            pltpu.SemaphoreType.DMA((12,)),
        ],
        3e9,
        far=(2, 3),
    )


def project_back_kernel(
    info, dq, own, other, tables, normed_t, residual, grad_hidden, gains, ffn_gain_grad, w, *refs
):
    input_grad, keep, send, g_s, by, back, spare, out_s, sems = refs
    core = info[0] % 2
    rows, width = dq.shape
    cosine, sine = tables[:, :LANES], tables[:, LANES:]
    sign = sine_signs(rows)
    low = lax.broadcasted_iota(jnp.int32, (rows, LANES), 1) < HEAD_SIZE

    def unturn(tile):
        return tile * cosine - turn(tile * sine, sign)

    for at in range(0, 2 * KV, LANES):
        tile = own[:, at : at + LANES] + other[:, at : at + LANES].astype(f32)
        if at + LANES <= KV:
            tile = unturn(tile)
        elif at < KV:
            tile = jnp.where(low, unturn(tile), tile)
        g_s[:, at : at + LANES] = tile.astype(bf16)
    for at in range(0, width, LANES):
        n = min(LANES, width - at)
        if n == LANES:
            tile = unturn(dq[:, at : at + LANES])
        else:
            half = dq[:, at : at + n]
            tile = unturn(jnp.concatenate([half, half], axis=1))[:, :n]
        g_s[:, 2 * KV + at : 2 * KV + at + n] = tile.astype(bf16)
    step = 2 * LANES
    for c in range(0, width, step):
        here = slice(c, min(c + step, width))
        back[:, here] = dot(g_s[...], w[here, :QKV], NT)
    through, gain_grad = norm_back(residual[...], gains[0:1, :], back[...])
    input_grad[...] = (grad_hidden[...] + through).astype(bf16)
    spare[...] = jnp.concatenate(
        [
            jnp.broadcast_to(gain_grad, (LANES // 2, width)),
            jnp.broadcast_to(ffn_gain_grad[0:1, :], (LANES // 2, width)),
        ],
        axis=0,
    ).T
    cols, kv_cols = width // 8, KV // 8
    first = cols + 2 * kv_cols
    by[...] = jnp.zeros_like(by)
    for y in range(2):
        for z in range(4):
            t, at = 2 * z + y, (4 * y + z) * step
            by[:, at : at + cols] = g_s[:, 2 * KV + t * cols : 2 * KV + (t + 1) * cols]
            at = at + cols
            by[:, at : at + kv_cols] = g_s[:, t * kv_cols : (t + 1) * kv_cols]
            at = at + kv_cols
            by[:, at : at + kv_cols] = g_s[:, KV + t * kv_cols : KV + (t + 1) * kv_cols]
    lane = lax.broadcasted_iota(jnp.int32, (width, step), 1)
    one, two = spare[:, 0:1], spare[:, LANES - 1 : LANES]
    for c in range(0, 8 * step, step):
        value = dot(normed_t[...], by[:, c : c + step])
        value = jnp.where(lane == first, one, value)
        out_s[:, c : c + step] = jnp.where(lane == first + 1, two, value).astype(bf16)
    copies = Copies(sems)
    for place in range(4):
        source = out_s.at[pl.ds(place * 240, 240), :]
        there = place // 2
        copies.keep_or_send(core, place % 2, source, keep.at[there], send.at[there])
    copies.wait()


def project_back(info, dq, own, other, tables, normed_t, residual, grad_hidden, gains, gain_grad, w):
    rows, width = dq.shape
    step = 2 * LANES
    return call(
        project_back_kernel,
        "project_back",
        [
            shaped((rows, width), bf16),
            shaped((2, 240, 8 * step), bf16),
            shaped((2, 240, 8 * step), bf16),
        ],
        [info, dq, own, other, tables, normed_t, residual, grad_hidden, gains, gain_grad, w],
        [SM] + [VM] * 10,
        [
            pltpu.VMEM((rows, QKV), bf16),
            pltpu.VMEM((rows, 8 * step), bf16),
            pltpu.VMEM((rows, width), f32),
            pltpu.VMEM((width, LANES), f32),
            pltpu.VMEM((width, 8 * step), bf16),
            pltpu.SemaphoreType.DMA((4,)),
        ],
        5e9,
        far=(1, 2),
    )


def shards_small(
    inputs,
    attn_gain,
    query_weight,
    key_projection_weight,
    value_projection_weight,
    out_weight,
    ffn_gain,
    gate_weight,
    up_weight,
    down_weight,
    positions,
    cotangent,
):
    seqs, _, _, block, width = inputs.shape
    lay = Layout(seqs)
    ff = gate_weight.shape[1]
    even = lay.t % 2 == 0
    member = lay.member.astype(jnp.int32).reshape(1)
    info = jnp.stack([lay.f, lay.sequence, lay.t % 2]).astype(jnp.int32)

    place = positions.reshape(seqs, 2, block, 1)
    tokens = inputs.reshape(seqs, 2, block, width)
    packed = jnp.concatenate(
        [tokens, (place // 128).astype(bf16), (place % 128).astype(bf16)], axis=-1
    )
    qkvg = jnp.concatenate(
        [
            key_projection_weight,
            value_projection_weight,
            query_weight,
            attn_gain[:, None],
            ffn_gain[:, None],
            jnp.zeros((attn_gain.shape[0], 62), bf16),
            out_weight,
        ],
        axis=1,
    )
    got = lay.receive(packed)
    far = swap(qkvg, "fsdp", 2)
    far, *got = lax.optimization_barrier((far, *got))
    qkvg_pieces = [qkvg, far, swap(qkvg, "fsdp", 1), swap(far, "fsdp", 1)]


    def ffn_part(h, *before):
        lanes = slice(h * ff // 2, (h + 1) * ff // 2)
        parts = gate_weight[:, lanes], up_weight[:, lanes]
        return after(jnp.concatenate(parts, axis=1), *before)

    far0 = swap(ffn_part(0, far), "fsdp", 2)

    residual, normed, normed_t, query, kv, tables, gains, w = project(info, got, qkvg_pieces, width)
    pieces = lay.gather_group(kv)
    grad_got = lay.receive(after(cotangent.reshape(seqs, 2, block, width), residual))
    far0, grad_got[0], grad_got[1], *pieces = lax.optimization_barrier(
        (far0, grad_got[0], grad_got[1], *pieces)
    )
    far0_o = swap(far0, "fsdp", 1)
    down_weight = after(down_weight.T, far0)
    down_far = swap(down_weight, "fsdp", 2)
    mixed, mixed_t, lse = attention_forward(member, query, pieces)
    mixed, *grad_got = lax.optimization_barrier((mixed, *grad_got))
    gate_weight, up_weight, down_weight = lax.optimization_barrier(
        (gate_weight, up_weight, down_weight, mixed)
    )[:3]
    far1 = swap(ffn_part(1, mixed), "fsdp", 2)
    gate_p = [gate_weight, swap(gate_weight, "fsdp", 1)]
    up_p = [up_weight, swap(up_weight, "fsdp", 1)]
    down_o = swap(down_weight, "fsdp", 1)
    hidden, normed_ffn, normed_ffn_t = branch(info, mixed, residual, gains, qkvg_pieces)
    grads, grads_by = order(info, grad_got)
    down_far, normed_ffn = lax.optimization_barrier((down_far, normed_ffn))
    down_far_o = swap(down_far, "fsdp", 1)
    down_p = [down_weight, down_o, down_far, down_far_o]

    sums = Sums()

    def over_core(keep, send):
        return add(keep, swap(send, "fsdp", 1))

    common = (info, normed_ffn, normed_ffn_t, grads, grads_by)
    result, back, keep0, send0 = ffn(
        0, *common, hidden, hidden, gate_p, up_p, down_p, [far0, far0_o]
    )
    far1, result = lax.optimization_barrier((far1, result))
    far1_o = swap(far1, "fsdp", 1)
    result, back, keep1, send1 = ffn(
        1, *common, result, back, gate_p, up_p, down_p, [far1, far1_o]
    )
    n = 2 * attn_gain.shape[0]
    core0 = over_core(keep0, send0)
    back, core0 = lax.optimization_barrier((back, core0))
    both0 = sums.over_x(core0[:n].reshape(2, n // 2, ff))
    grad_hidden, grad_mixed, out_k, out_s, ffn_gain_grad = branch_back(
        info, hidden, back, grads, mixed_t, gains, qkvg_pieces
    )
    core1 = over_core(keep1, send1)
    result = after(result, back)
    home = [lay.send_back(result, 0)]
    grad_mixed, core1 = lax.optimization_barrier((grad_mixed, core1))
    both1 = sums.over_y(core1[:n].reshape(2, n // 2, ff))
    down_sum = sums.halves(core0[n:], core1[n:], sums.x, "fsdp", 2)
    dq, dkv, dkv_send = attention_backward(member, query, pieces, mixed, grad_mixed, lse)
    dkv_other = lay.around(dkv_send, 1)
    dq, both0, both1, down_sum, result, *home = lax.optimization_barrier(
        (dq, both0, both1, down_sum, result, *home)
    )
    both0 = sums.over_y(both0)
    both1 = sums.over_x(both1)
    home += [lay.send_back(result, r) for r in range(1, seqs)]
    input_grad, qkv_k, qkv_s = project_back(
        info, dq, dkv, dkv_other, tables, normed_t, residual, grad_hidden, gains, ffn_gain_grad, w
    )
    qkv_s, out_s, *home = lax.optimization_barrier((qkv_s, out_s, *home))
    outputs = lay.place_back(home)
    qkv_sum = over_core(qkv_k, qkv_s)
    out_sum = over_core(out_k, out_s)
    qkv_sum, out_sum, both0, both1, down_sum = lax.optimization_barrier(
        (qkv_sum, out_sum, both0, both1, down_sum)
    )
    qkv_sum = sums.over_x(qkv_sum)
    out_sum = sums.over_y(out_sum)
    qkv_sum, out_sum, down_sum, input_grad = lax.optimization_barrier(
        (qkv_sum, out_sum, down_sum, input_grad)
    )
    down_sum = sums.over_y(down_sum)
    out_sum = sums.over_x(out_sum)
    input_grad = lay.from_sequence(input_grad)
    cols, kv_cols, ff_cols = width // 8, KV // 8, ff // 8
    half = 2 * ff_cols
    gate_up = sums.over_z(
        jnp.stack([b[:, i * half : (i + 1) * half] for b in (both0, both1) for i in range(2)])
    )
    qkv_sum = sums.over_y(qkv_sum)
    pieces = []
    for z in range(4):
        low = out_sum[:, z * LANES : (z + 1) * LANES]
        low = jnp.concatenate([low[i * 48 : (i + 1) * 48] for i in range(5)], axis=1)
        part = down_sum[z % 2 * LANES : (z % 2 + 1) * LANES, z // 2 * half : (z // 2 + 1) * half]
        wide = qkv_sum[:, 2 * z * LANES : 2 * (z + 1) * LANES]
        last = jnp.concatenate([wide[192:, :LANES], wide[192:, LANES:]])
        wide = jnp.concatenate([wide[:96], wide[96:192], last], axis=1)
        pieces.append(jnp.concatenate([part, low, wide]))
    rest = sums.over_z(jnp.stack(pieces))
    first = cols + 2 * kv_cols
    low, wide = rest[LANES : LANES + 48], rest[LANES + 48 :]
    out_grad = jnp.concatenate([low[:, i * LANES : i * LANES + cols] for i in range(5)])
    step = 2 * LANES
    last = jnp.concatenate([wide[:48, 2 * step :], wide[48:, 2 * step :]], axis=1)
    qkv_sum = jnp.concatenate([wide[:, :step], wide[:, step : 2 * step], last])
    return (
        outputs.reshape(inputs.shape),
        input_grad.astype(f32).reshape(inputs.shape),
        qkv_sum[:, first],
        qkv_sum[:, :cols],
        qkv_sum[:, cols : cols + kv_cols],
        qkv_sum[:, cols + kv_cols : first],
        out_grad,
        qkv_sum[:, first + 1],
        gate_up[:, :ff_cols],
        gate_up[:, ff_cols:],
        rest[:cols].T,
    )


def shards(
    inputs,
    attn_gain,
    query_weight,
    key_projection_weight,
    value_projection_weight,
    out_weight,
    ffn_gain,
    gate_weight,
    up_weight,
    down_weight,
    positions,
    cotangent,
):
    seqs, _, _, block, width = inputs.shape
    lay = Layout(seqs)
    place = positions.reshape(seqs, 2, block, 1)
    packed = jnp.concatenate(
        [
            inputs.reshape(seqs, 2, block, width),
            (place // 128).astype(bf16),
            (place % 128).astype(bf16),
        ],
        axis=-1,
    )
    packed = lay.to_sequence(packed)
    residual = packed[:, :width].astype(f32)
    place = packed[:, width].astype(f32) * 128.0 + packed[:, width + 1].astype(f32)
    member = lay.member.astype(jnp.int32).reshape(1)
    qkvg = jnp.concatenate(
        [
            query_weight,
            key_projection_weight,
            value_projection_weight,
            attn_gain[:, None],
            ffn_gain[:, None],
        ],
        axis=1,
    )
    qkvg_full, out_full, gate_full, up_full, down_full = [
        lax.all_gather(w, "fsdp", axis=0, tiled=True)
        for w in (qkvg, out_weight, gate_weight, up_weight, down_weight)
    ]
    qkv_full = qkvg_full[:, : width + 2 * KV]
    first_gain = qkvg_full[:, width + 2 * KV].astype(f32)
    second_gain = qkvg_full[:, width + 2 * KV + 1].astype(f32)

    cosine, sine = rope_tables(place)
    normalized, inverse_first = norm_forward(residual, first_gain)
    normed = normalized.astype(bf16)
    qkv = dot(normed, qkv_full)
    query = rotate_pairs(qkv[:, :width], cosine, sine).astype(bf16)
    keys = rotate_pairs(qkv[:, width : width + KV], cosine, sine).astype(bf16)
    values = qkv[:, width + KV :].astype(bf16)
    pieces = lay.gather_group(jnp.concatenate([keys, values], axis=1))
    grad_rows = lay.to_sequence(cotangent.reshape(seqs, 2, block, width))
    mixed, _, lse = attention_forward(member, query, pieces)
    hidden = residual + dot(mixed, out_full)
    normed_ffn, inverse_second = norm_forward(hidden, second_gain)
    normed_ffn = normed_ffn.astype(bf16)
    gate = dot(normed_ffn, gate_full)
    up = dot(normed_ffn, up_full)
    sigmoid = jax.nn.sigmoid(gate)
    act = (gate * sigmoid * up).astype(bf16)
    outputs = lay.from_sequence((hidden + dot(act, down_full)).astype(bf16))
    down_grad = dot(act, grad_rows, TN).astype(bf16)
    grad_act = dot(grad_rows, down_full, NT)
    grad_up = (grad_act * gate * sigmoid).astype(bf16)
    grad_gate = (grad_act * up * sigmoid * (1.0 + gate * (1.0 - sigmoid))).astype(bf16)
    gate_grad = dot(normed_ffn, grad_gate, TN).astype(bf16)
    up_grad = dot(normed_ffn, grad_up, TN).astype(bf16)
    grad_normed_ffn = dot(grad_gate, gate_full, NT) + dot(grad_up, up_full, NT)
    through, ffn_gain_grad = norm_backward(hidden, inverse_second, second_gain, grad_normed_ffn)
    grad_hidden = grad_rows.astype(f32) + through
    grad_branch = grad_hidden.astype(bf16)
    out_grad = dot(mixed, grad_branch, TN).astype(bf16)
    grad_mixed = dot(grad_branch, out_full, NT).astype(bf16)
    dq, dkv, *sends = attention_backward(member, query, pieces, mixed, grad_mixed, lse)
    dkv = lay.scatter_group(dkv, sends)
    grad_qkv = jnp.concatenate(
        [
            rotate_pairs_back(dq, cosine, sine).astype(bf16),
            rotate_pairs_back(dkv[:, :KV], cosine, sine).astype(bf16),
            dkv[:, KV:].astype(bf16),
        ],
        axis=1,
    )
    grad_normed = dot(grad_qkv, qkv_full, NT)
    grad_input, attn_gain_grad = norm_backward(residual, inverse_first, first_gain, grad_normed)
    input_grad = lay.from_sequence((grad_hidden + grad_input).astype(bf16))
    qkv_grad = dot(normed, grad_qkv, TN).astype(bf16)

    def scatter(grads):
        part = lax.psum_scatter(grads, "fsdp", scatter_dimension=0, tiled=True)
        return lax.psum_scatter(part, "ctx", scatter_dimension=1, tiled=True).astype(f32)

    down_grad, gate_grad, up_grad, out_grad, query_grad, key_grad, value_grad = [
        scatter(g)
        for g in (
            down_grad,
            gate_grad,
            up_grad,
            out_grad,
            qkv_grad[:, :width],
            qkv_grad[:, width : width + KV],
            qkv_grad[:, width + KV :],
        )
    ]
    gains = lax.psum(jnp.stack([attn_gain_grad, ffn_gain_grad]), ("ctx", "fsdp"))
    gain_rows = attn_gain.shape[0]
    gains = lax.dynamic_slice_in_dim(gains, lay.f * gain_rows, gain_rows, 1)
    return (
        outputs.reshape(inputs.shape),
        input_grad.astype(f32).reshape(inputs.shape),
        gains[0],
        query_grad,
        key_grad,
        value_grad,
        out_grad,
        gains[1],
        gate_grad,
        up_grad,
        down_grad,
    )


def solution(mesh):
    in_specs = (
        P("fsdp", "ctx", None, None, None),
        P("fsdp"),
        P("fsdp", None),
        P("fsdp", None),
        P("fsdp", None),
        P("fsdp", None),
        P("fsdp"),
        P("fsdp", None),
        P("fsdp", None),
        P("fsdp", None),
        P("fsdp", "ctx", None, None),
        P("fsdp", "ctx", None, None, None),
    )
    out_specs = (
        P("fsdp", "ctx", None, None, None),
        P("fsdp", "ctx", None, None, None),
        P("fsdp"),
        P("fsdp", "ctx"),
        P("fsdp", "ctx"),
        P("fsdp", "ctx"),
        P("fsdp", "ctx"),
        P("fsdp"),
        P("fsdp", "ctx"),
        P("fsdp", "ctx"),
        P("fsdp", "ctx"),
    )
    small = mesh.shape["fsdp"] == 4 and mesh.shape["ctx"] == 8
    return jax.shard_map(
        shards_small if small else shards, mesh=mesh, in_specs=in_specs, out_specs=out_specs, check_vma=False)
```
